512 devices in a mesh: grp: 16 (over z, core), dev: 32 (over y, x).
Axes of the slice: x: 4, y: 8, z: 8, core: 2. Of those that a mesh axis runs over, the one named last changes fastest.
Arguments:
- queries: bfloat16 [8192, 768], P(('grp', 'dev')), may hold values from -32 to 32
- passages: bfloat16 [1048576, 768], P(('grp', 'dev')), may hold values from -16 to 16
- list_tiles: int32 [512], P(('grp', 'dev')), may hold values from 1 to 16, 5120 in all
- probes: int32 [8192, 32], P(('grp', 'dev')), may hold values from 0 to 511, all different within a row; in each aligned block of 16 rows (0 to 15, 16 to 31, ...) at most 2 rows name the same one
- fb_probe: int32 [8192, 10], P(('grp', 'dev')), may hold values from 0 to 31, all different within a row
- fb_row: int32 [8192, 10], P(('grp', 'dev')), may hold values from 0 to 127
Outputs:
- retrieved: bfloat16 [8192, 768], P(('grp', 'dev'))
- log_total: float32 [8192], P(('grp', 'dev'))
The draws below stay inside these ranges and needn't reach their ends.
Inputs may be any that keep to these rules, and one draw needn't show every extreme that they name: `probes`: in each aligned block of 16 queries (the queries of one device) no list is probed by more than 2 of them, a bound that some block reaches; the lists of one query are distinct. The live rows of list l are its first 128 * list_tiles[l] rows; the live tiles of all lists add up to 5120, and some list has all 16. `fb_probe`: the 10 positions of one query are distinct.
All inputs are finite; a program needn't handle non-finite values. No bound on the sum of `list_tiles` on one device may be relied on, other than what follows from the above.
Results may differ from the reference program's by a relative error of at most 0.0071.
Values may be sent and summed in bfloat16 or wider, within the bound.
A program may use at most 64 MiB of HBM per device.

```python
import math
import jax
import jax.numpy as jnp
import numpy as np
from jax import lax

D = 768
ROWS_LIST = 2048
TILE = 128
FB = 10
Q_DEV = 16
TILES_LIST = 16
LISTS = 512
PROBES = 32
CAP = 2
QUERIES = 8192
TILE_TOTAL = 5120
N_GRP = 16
N_DEV = 32


def draw_queries(key, part):
    base_key = jax.random.fold_in(key, 11)
    values = jax.random.normal(base_key, (QUERIES, D), jnp.float32)
    return jnp.clip(values, -32.0, 32.0).astype(jnp.bfloat16)


def draw_passages(key, part):
    base_key = jax.random.fold_in(key, 23)
    row_total = LISTS * ROWS_LIST
    values = jax.random.normal(base_key, (row_total, D), jnp.float32)
    return jnp.clip(values, -16.0, 16.0).astype(jnp.bfloat16)


def set_ends(array, key, smallest, high):
    longest = array.shape.index(max(array.shape))
    spots = []
    for shift in (0, 1):
        where = [jax.random.randint(jax.random.fold_in(key, axis), (), 0, length) for axis, length in enumerate(array.shape)]
        where[longest] = (where[longest] + shift) % array.shape[longest]
        spots.append(tuple(where))
    return array.at[spots[0]].set(smallest).at[spots[1]].set(high)


def choose_distinct(rng, rows, amount, top, lift):
    ranking = jax.random.permutation(jax.random.fold_in(rng, 1), amount)
    boost = ranking
    for power in range(3):
        boost = boost * boost // amount
    boost = boost * lift // amount
    tickets = jax.random.randint(jax.random.fold_in(rng, 2), (rows, amount), 0, 4096) + boost
    fixed_rows = jax.random.permutation(jax.random.fold_in(rng, 3), rows)[jnp.arange(amount) % rows]
    tickets = jnp.where(jnp.arange(rows)[:, None] == fixed_rows[None, :], 1 << 14, tickets)
    merit = tickets * amount + jnp.arange(amount)
    return lax.top_k(merit.astype(jnp.int32), top)[1].astype(jnp.int32)


def length_profile(amount, total, most, skew):
    weights = [(1 << 20) // math.isqrt(standing ** skew) + 1 for standing in range(2, amount + 1)]
    spare, counts = total - most - (amount - 1), [1] * (amount - 1)
    while spare > 0:
        candidates = [i for i in range(amount - 1) if counts[i] < most]
        mass, budget = sum([weights[i] for i in candidates]), spare
        for i in candidates:
            more = min(most - counts[i], max(1, budget * weights[i] // mass), spare)
            counts[i] = counts[i] + more
            spare = spare - more
    return np.array([most] + counts)


def uneven(stream_key, amount, total, bound, skew):
    if amount == 2:
        one = jax.random.randint(stream_key, (), max(1, total - bound), min(bound, total - 1) + 1)
        return jnp.stack([one, total - one])
    tallies = jnp.asarray(length_profile(amount, total, bound, skew), jnp.int32)
    pairs = (amount - 1) // 2
    source_of, sink = tallies[1:1 + 2 * pairs:2], tallies[2:2 + 2 * pairs:2]
    margin = jnp.minimum(source_of - 1, bound - sink)
    passed = jax.random.randint(jax.random.fold_in(stream_key, 1), (pairs,), 0, 1 << 20) % (margin + 1)
    tallies = tallies.at[1:1 + 2 * pairs:2].set(source_of - passed).at[2:2 + 2 * pairs:2].set(sink + passed)
    return tallies[jax.random.permutation(jax.random.fold_in(stream_key, 2), amount)]


def routed_block(key, own, number, rows, number_of, top, reach, lean):
    ranking = jax.random.permutation(key, number_of)
    crowded, ordinary = shares(number_of, rows * top, reach, lean, True), shares(number_of, rows * top, reach, lean, False)
    places = jnp.arange(number_of)

    def named(tallies, turn):
        used = int((tallies > 0).sum())
        fixed = max(1, used // 4)
        shifted = fixed + (places - fixed + turn * (used - fixed)) % max(1, number_of - fixed)
        return jnp.zeros((number_of,), jnp.int32).at[ranking[jnp.where(places < fixed, places, shifted)]].set(jnp.asarray(tallies, jnp.int32))

    tallies = jnp.where(number % 4 == 0, named(crowded, number // 4), named(ordinary, number - number // 4 - 1))
    mixed = jax.random.permutation(jax.random.fold_in(own, 3), number_of)
    source_of, receiver = mixed[0:number_of // 2 * 2:2], mixed[1:number_of // 2 * 2:2]
    slack = jnp.minimum(tallies[source_of] - 1, reach - tallies[receiver]) // 2
    slack = jnp.where((source_of == ranking[0]) | (receiver == ranking[0]) | (tallies[receiver] == 0), 0, jnp.maximum(slack, 0))
    shifted = jax.random.randint(jax.random.fold_in(own, 4), (number_of // 2,), 0, 1 << 20) % (slack + 1)
    tallies = tallies.at[source_of].add(-shifted).at[receiver].add(shifted)
    members = jnp.searchsorted(jnp.cumsum(tallies), jnp.arange(rows * top), side="right").astype(jnp.int32)
    grid = members.reshape(top, rows).T
    grid = grid[jax.random.permutation(jax.random.fold_in(own, 1), rows)]
    turn = jax.random.randint(jax.random.fold_in(own, 2), (rows, 1), 0, top)
    return jnp.take_along_axis(grid, (jnp.arange(top)[None, :] + turn) % top, axis=1)


def shares(amount, total, reach, skew, full):
    loads = [(1 << 20) // math.isqrt(rank ** skew) + 1 for rank in range(1, amount + 1)]
    largest = reach if full else min(reach, max(-(-total // amount), total * loads[0] // sum(loads)))
    least = 1 if total - largest >= amount - 1 else 0
    holding, surplus = [largest] + [least] * (amount - 1), total - largest - least * (amount - 1)
    while surplus > 0:
        free = [i for i in range(1, amount) if holding[i] < largest] or [i for i in range(1, amount) if holding[i] < reach]
        whole, budget = sum([loads[i] for i in free]), surplus
        for i in free:
            extra = min(reach - holding[i], max(1, budget * loads[i] // whole), surplus)
            holding[i] = holding[i] + extra
            surplus = surplus - extra
    return np.array(holding)


def setup_inputs(seed: int = 0) -> dict:
    key_of = jax.random.split(jax.random.key(seed), 7)
    queries = draw_queries(jax.random.fold_in(key_of[6], 71), 0)
    passages = draw_passages(jax.random.fold_in(key_of[6], 71), 0)
    list_tiles = uneven(key_of[2], LISTS, TILE_TOTAL, TILES_LIST, 2).astype(jnp.int32)
    probes_keys = jax.random.split(jax.random.fold_in(key_of[3], 1), QUERIES // Q_DEV)
    probes_turns = jax.random.permutation(jax.random.fold_in(key_of[3], 3), QUERIES // Q_DEV)
    probes = jax.vmap(lambda own, number: routed_block(jax.random.fold_in(key_of[3], 2), own, number, Q_DEV, LISTS, PROBES, CAP, 2))(probes_keys, probes_turns).reshape((QUERIES, PROBES))
    fb_probe = choose_distinct(key_of[4], QUERIES, PROBES, FB, 0)
    fb_row = set_ends(jax.random.randint(key_of[5], (QUERIES, FB), 0, TILE), jax.random.fold_in(key_of[5], 1), 0, TILE - 1).astype(jnp.int32)
    return {"queries": queries, "passages": passages, "list_tiles": list_tiles, "probes": probes, "fb_probe": fb_probe, "fb_row": fb_row}


ALPHA_WEIGHT = 1.0
BETA_WEIGHT = 0.75
NEG_FILL = -1e+30

def probe_ranks(block_lists):
    flat_lists = block_lists.reshape(-1)
    position = jnp.arange(flat_lists.shape[0], dtype=jnp.int32)
    same_list = flat_lists[:, None] == flat_lists[None, :]
    earlier = position[:, None] > position[None, :]
    return lax.optimization_barrier(jnp.sum(jnp.logical_and(same_list, earlier), axis=1)).astype(jnp.int32)

def reference(queries, passages, list_tiles, probes, fb_probe, fb_row):
    block_count = N_GRP * N_DEV
    fb_list = jnp.take_along_axis(probes, fb_probe, axis=1)
    fb_index = (fb_list * ROWS_LIST + fb_row).astype(jnp.int32)
    fb_rows = jnp.take(passages, fb_index.reshape(-1), axis=0).astype(jnp.float32).reshape(QUERIES, FB, D)
    fb_mean = lax.optimization_barrier(jnp.sum(fb_rows, axis=1)) / FB
    rocchio = (ALPHA_WEIGHT * queries.astype(jnp.float32) + BETA_WEIGHT * fb_mean).astype(jnp.bfloat16)
    ranks_all = lax.map(probe_ranks, probes.reshape(block_count, Q_DEV * PROBES))
    item_query = jnp.arange(QUERIES * PROBES, dtype=jnp.int32) // PROBES
    item_block = item_query // Q_DEV
    slot_index = (probes.reshape(-1) * block_count + item_block) * CAP + ranks_all.reshape(-1)
    slot_query = jnp.full((LISTS * block_count * CAP,), -1, jnp.int32).at[slot_index].set(item_query)
    score_scale = 3.0 / math.sqrt(D)
    row_position = jnp.arange(ROWS_LIST, dtype=jnp.int32)

    def score_list(inputs_list):
        list_number, tile_count, owners = inputs_list
        list_rows = lax.dynamic_slice_in_dim(passages, (list_number * ROWS_LIST).astype(jnp.int32), ROWS_LIST, 0)
        vectors = jnp.take(rocchio, jnp.maximum(owners, 0), axis=0)
        scores = jnp.dot(vectors, list_rows.T, preferred_element_type=jnp.float32) * score_scale
        scores = jnp.where(row_position[None, :] < tile_count * TILE, scores, NEG_FILL)
        score_peak = lax.optimization_barrier(jnp.max(scores, axis=1))
        weights = jnp.exp(scores - score_peak[:, None])
        score_mass = lax.optimization_barrier(jnp.sum(weights, axis=1))
        partial_value = jnp.dot(weights.astype(jnp.bfloat16), list_rows, preferred_element_type=jnp.float32)
        return (partial_value, score_peak, score_mass)
    partials, peaks, masses = lax.map(score_list, (jnp.arange(LISTS, dtype=jnp.int32), list_tiles, slot_query.reshape(LISTS, block_count * CAP)))
    owners = slot_query.reshape(-1)
    is_live = owners >= 0
    segment_index = jnp.maximum(owners, 0)
    live_peaks = jnp.where(is_live, peaks.reshape(-1), NEG_FILL)
    query_peak = jnp.maximum(jax.ops.segment_max(live_peaks, segment_index, num_segments=QUERIES), NEG_FILL)
    factor = jnp.where(is_live, jnp.exp(live_peaks - jnp.take(query_peak, segment_index)), 0.0)
    query_mass = jax.ops.segment_sum(factor * masses.reshape(-1), segment_index, num_segments=QUERIES)

    def add_list(summed, inputs_list):
        partial_value, list_factor, list_index = inputs_list
        return (summed.at[list_index].add(list_factor[:, None] * partial_value), None)
    summed, _ = lax.scan(add_list, jnp.zeros((QUERIES, D), jnp.float32), (partials, factor.reshape(LISTS, -1), segment_index.reshape(LISTS, -1)))
    retrieved = (summed / query_mass[:, None]).astype(jnp.bfloat16)
    log_total = query_peak + jnp.log(query_mass)
    return (retrieved, log_total)
```

```python
import functools
import math

import jax
import jax.numpy as jnp
from jax import lax
from jax.experimental import pallas as pl
from jax.experimental.pallas import tpu as pltpu
from jax.sharding import PartitionSpec as P

TILE = 128
SLOTS = 2
CORES = 2
LANES = 128
ALPHA_WEIGHT = 1.0
BETA_WEIGHT = 0.75
NEG_FILL = -1e30
F32 = jnp.float32
BF16 = jnp.bfloat16
MESH = pl.DeviceIdType.MESH


def iota(shape, dim):
    return lax.broadcasted_iota(jnp.int32, shape, dim)


def kernel(
    sizes,
    queries_ref,
    probes_ref,
    fb_probe_ref,
    fb_row_ref,
    tiles_ref,
    passages_ref,
    retrieved_ref,
    log_ref,
    held,
    table,
    table_in,
    asked,
    asked_in,
    owner_row,
    select,
    found,
    found_in,
    fsum,
    fsum_in,
    roc,
    roc_in,
    vec,
    vec_in,
    part,
    part_in,
    lse,
    lse_in,
    comb,
    comb_in,
    lse2,
    lse2_in,
    held_sem,
    send_sem,
    recv_sem,
    vec_sem,
):
    groups, members, rows, queries, probe_count, fb_count, width = sizes
    ring = groups // CORES
    across = members // ring
    lists = groups * members
    half = width // 2
    blocks = groups
    slab = SLOTS * blocks
    plane = members
    chunk = ring * slab
    held_queries = blocks * queries
    slots = plane * slab
    tile_lanes = min(LANES, slots)
    per_tile = tile_lanes // slab

    grp, dev = lax.axis_index("grp"), lax.axis_index("dev")
    z, c = grp // CORES, grp % CORES
    y, x = dev // across, dev % across
    my_b = (grp, y * CORES + c)
    my_o = (y, z)
    my_k = (x * ring + y, x * ring + z)

    def outer_id(r, b):
        if r == 0:
            return (b, dev)
        return (z * CORES + b % CORES, (b // CORES) * across + x)

    def plane_id(r, k):
        far_x, far_o = k // ring, k % ring
        if r == 0:
            return (grp, far_o * across + far_x)
        return (far_o * CORES + c, y * across + far_x)

    def to_outer(r, phase, source, target):
        pltpu.make_async_copy(source(my_b[r]), target.at[r, my_b[r]], recv_sem.at[r, phase]).start()

        @pl.loop(1, blocks)
        def _(i):
            b = (my_b[r] + i) % blocks
            pltpu.make_async_remote_copy(
                src_ref=source(b),
                dst_ref=target.at[r, my_b[r]],
                send_sem=send_sem.at[r, phase],
                recv_sem=recv_sem.at[r, phase],
                device_id=outer_id(r, b),
                device_id_type=MESH,
            ).start()

    def to_plane(r, phase, source, target):
        mine = my_k[r]
        pltpu.make_async_copy(source.at[r, mine], target.at[r, mine], recv_sem.at[r, phase]).start()

        @pl.loop(1, plane)
        def _(i):
            k = (mine + i) % plane
            pltpu.make_async_remote_copy(
                src_ref=source.at[r, k],
                dst_ref=target.at[r, mine],
                send_sem=send_sem.at[r, phase],
                recv_sem=recv_sem.at[r, phase],
                device_id=plane_id(r, k),
                device_id_type=MESH,
            ).start()

    def arrived(r, phase, target):
        pltpu.make_async_copy(target.at[r], target.at[r], recv_sem.at[r, phase]).wait()

    def sent(r, phase, target):
        gone = target.at[r, pl.ds(1, target.shape[1] - 1)]
        pltpu.make_async_copy(gone, gone, send_sem.at[r, phase]).wait()

    copy_held = pltpu.make_async_copy(passages_ref, held, held_sem)
    copy_held.start()

    probes = probes_ref[...]
    fb_probe, fb_row = fb_probe_ref[...], fb_row_ref[...]
    position = iota((queries, probe_count), 1)
    wanted = jnp.ones((queries, probe_count), jnp.int32)
    for k in range(fb_count):
        wanted = jnp.where(position == fb_probe[:, k : k + 1], fb_row[:, k : k + 1] + 2, wanted)
    list_lane = iota((queries, lists), 1)
    named = jnp.zeros((queries, lists), jnp.int32)
    for j in range(probe_count):
        named = jnp.where(list_lane == probes[:, j : j + 1], wanted[:, j : j + 1], named)
    member = named > 0
    before = jnp.where(iota((queries, queries), 0) > iota((queries, queries), 1), 1.0, 0.0)
    rank = jnp.dot(
        before.astype(BF16),
        jnp.where(member, 1.0, 0.0).astype(BF16),
        preferred_element_type=F32,
    )
    code = (iota((queries, lists), 0) + 1) * 256 + named
    code = jnp.where(member, code, 0)
    for s in range(SLOTS):
        row = jnp.sum(jnp.where(rank == float(s), code, 0), axis=0, keepdims=True)
        table[0:1, s * lists : (s + 1) * lists] = row
    for r in range(2):
        to_outer(r, 0, lambda b: table, table_in)

    sub_b = iota((blocks, SLOTS * lists), 0)
    lane_l = iota((blocks, lists), 1)
    block_of = iota((slab, 1), 0) % blocks
    turn = iota((slab, LANES), 0) == iota((slab, LANES), 1) % slab
    query_lane = iota((slab, held_queries), 1)
    for r in range(2):
        arrived(r, 0, table_in)
        all_codes = jnp.zeros((blocks, SLOTS * lists), jnp.int32)
        for b in range(blocks):
            all_codes = jnp.where(sub_b == b, table_in[r, b], all_codes)

        @pl.loop(0, plane)
        def _(k, all_codes=all_codes, r=r):
            far_grp, far_dev = plane_id(r, k)
            here = lane_l == far_grp * members + far_dev
            columns = [
                jnp.sum(
                    jnp.where(here, all_codes[:, s * lists : (s + 1) * lists], 0),
                    axis=1,
                    keepdims=True,
                )
                for s in range(SLOTS)
            ]
            column = jnp.concatenate(columns, axis=0)
            owner = column >> 8
            want = (column & 255) - 2
            index = jnp.where(owner > 0, block_of * queries + owner - 1, -1)
            select[r, k] = jnp.where(query_lane == index, 1.0, 0.0).astype(BF16)
            asked[r, k] = jnp.sum(jnp.where(turn, want, 0), axis=0, keepdims=True)
            owner_row[r, k] = jnp.sum(jnp.where(turn, index, 0), axis=0, keepdims=True)

        to_plane(r, 1, asked, asked_in)

    tile_source = iota((1, tile_lanes), 1) // slab
    copy_held.wait()

    def lane_tile(ref, r, j):
        row = ref[r, per_tile * j][:, :tile_lanes]
        for i in range(1, per_tile):
            row = jnp.where(tile_source == i, ref[r, per_tile * j + i][:, :tile_lanes], row)
        return row

    for r in range(2):
        arrived(r, 1, asked_in)
        first = held[0:TILE, r * half : (r + 1) * half]
        for j in range(plane // per_tile):
            row = lane_tile(asked_in, r, j)
            hot = jnp.where(iota((TILE, tile_lanes), 0) == row, 1.0, 0.0).astype(BF16)
            picked = lax.dot_general(
                hot, first, (((0,), (0,)), ((), ())), preferred_element_type=F32
            ).astype(BF16)
            found[r, per_tile * j : per_tile * (j + 1)] = picked.reshape(per_tile, slab, half)
        to_plane(r, 2, found, found_in)

    for r in range(2):
        arrived(r, 2, found_in)
        total = lax.dot_general(
            select[r].reshape(slots, held_queries),
            found_in[r].reshape(slots, half),
            (((0,), (0,)), ((), ())),
            preferred_element_type=F32,
        )
        fsum[r] = total.astype(BF16).reshape(blocks, queries, half)
        to_outer(r, 3, lambda b, r=r: fsum.at[r, b], fsum_in)

    for r in range(2):
        arrived(r, 3, fsum_in)
        total = jnp.zeros((queries, half), F32)
        for b in range(blocks):
            total = total + fsum_in[r, b].astype(F32)
        own = queries_ref[:, r * half : (r + 1) * half].astype(F32)
        roc[r] = (ALPHA_WEIGHT * own + BETA_WEIGHT * (total / fb_count)).astype(BF16)
        to_outer(r, 4, lambda b, r=r: roc.at[r], roc_in)

    for r in range(2):
        arrived(r, 4, roc_in)

    @pl.loop(0, across)
    def _(t):
        far_x = (x + across - t) % across
        for r in range(2):
            vectors = roc_in[r].reshape(held_queries, half)
            there = pl.ds(far_x * ring, ring)
            picked = jnp.dot(
                select[r, there].reshape(chunk, held_queries),
                vectors,
                preferred_element_type=F32,
            )
            vec[r, there] = picked.astype(BF16).reshape(ring, slab, half)

            @pl.when(t == 0)
            def _():
                pltpu.make_async_copy(
                    vec.at[r, my_k[r]], vec_in.at[r, my_k[r]], vec_sem.at[r, x]
                ).start()

            @pl.loop(0, ring)
            def _(i):
                k = far_x * ring + (my_o[r] + i) % ring

                @pl.when(t + i > 0)
                def _():
                    pltpu.make_async_remote_copy(
                        src_ref=vec.at[r, k],
                        dst_ref=vec_in.at[r, my_k[r]],
                        send_sem=send_sem.at[r, 5],
                        recv_sem=vec_sem.at[r, x],
                        device_id=plane_id(r, k),
                        device_id_type=MESH,
                    ).start()

    scale = 3.0 / math.sqrt(width)
    live = tiles_ref[0] * TILE
    bits = slab // 2

    def swapped(index):
        o, s, low = index // slab, (index % slab) // bits, index % bits
        return (low // CORES) * slab + s * bits + o * CORES + low % CORES

    swap = jnp.where(
        iota((chunk, chunk), 0) == swapped(iota((chunk, chunk), 1)), 1.0, 0.0
    ).astype(BF16)

    @pl.loop(0, across)
    def _(t):
        far_x = (x + t) % across
        there = pl.ds(far_x * ring, ring)
        for r in range(2):
            landed = vec_in.at[r, there]
            pltpu.make_async_copy(landed, landed, vec_sem.at[r, far_x]).wait()
        first = vec_in[0, there].reshape(chunk, half)
        second = jnp.dot(
            swap, vec_in[1, there].reshape(chunk, half), preferred_element_type=F32
        ).astype(BF16)
        contract = (((1,), (1,)), ((), ()))
        scores = lax.dot_general(first, held[:, :half], contract, preferred_element_type=F32)
        scores = scores + lax.dot_general(
            second, held[:, half:], contract, preferred_element_type=F32
        )
        scores = jnp.where(iota((chunk, rows), 1) < live, scores * scale, NEG_FILL)
        peak = jnp.max(scores, axis=1, keepdims=True)
        weights = jnp.exp(scores - peak)
        mass = jnp.sum(weights, axis=1, keepdims=True)
        value = jnp.dot(weights.astype(BF16), held[...], preferred_element_type=F32)
        value = (value / mass).astype(BF16)
        level = peak + jnp.log(mass)
        part[0, there] = value[:, :half].reshape(ring, slab, half)
        part[1, there] = (
            jnp.dot(swap, value[:, half:], preferred_element_type=F32)
            .astype(BF16)
            .reshape(ring, slab, half)
        )
        sub, lane = iota((chunk, LANES), 0), iota((chunk, LANES), 1) % slab
        for o in range(ring):
            for r in range(2):
                place = o * slab + lane
                if r == 1:
                    place = swapped(place)
                row = jnp.sum(jnp.where(sub == place, level, 0.0), axis=0, keepdims=True)
                lse[r, far_x * ring + o] = row
        for r in range(2):

            @pl.when(t == 0)
            def _():
                for source, target, phase in ((lse, lse_in, 7), (part, part_in, 6)):
                    pltpu.make_async_copy(
                        source.at[r, my_k[r]], target.at[r, my_k[r]], recv_sem.at[r, phase]
                    ).start()

            @pl.loop(0, ring)
            def _(i):
                k = far_x * ring + (my_o[r] + i) % ring

                @pl.when(t + i > 0)
                def _():
                    for source, target, phase in ((lse, lse_in, 7), (part, part_in, 6)):
                        pltpu.make_async_remote_copy(
                            src_ref=source.at[r, k],
                            dst_ref=target.at[r, my_k[r]],
                            send_sem=send_sem.at[r, phase],
                            recv_sem=recv_sem.at[r, phase],
                            device_id=plane_id(r, k),
                            device_id_type=MESH,
                        ).start()

    sub_q = iota((held_queries, tile_lanes), 0)
    for r in range(2):
        arrived(r, 7, lse_in)
        levels, masks = [], []
        for j in range(plane // per_tile):
            masks.append(sub_q == lane_tile(owner_row, r, j))
            levels.append(jnp.where(masks[-1], lane_tile(lse_in, r, j), NEG_FILL))
        levels = jnp.concatenate(levels, axis=1)
        mask = jnp.concatenate([jnp.where(m, 1.0, 0.0) for m in masks], axis=1)
        top = jnp.max(levels, axis=1, keepdims=True)
        weights = jnp.exp(levels - top) * mask
        total = jnp.sum(weights, axis=1, keepdims=True)
        high = weights.astype(BF16)
        low = (weights - high.astype(F32)).astype(BF16)
        arrived(r, 6, part_in)
        parts = part_in[r].reshape(slots, half)
        value = jnp.dot(high, parts, preferred_element_type=F32)
        value = value + jnp.dot(low, parts, preferred_element_type=F32)
        some = total > 0.0
        total = jnp.where(some, total, 1.0)
        comb[r] = (value / total).astype(BF16).reshape(blocks, queries, half)
        level = jnp.where(some, top + jnp.log(total), NEG_FILL)
        sub, lane = iota((held_queries, LANES), 0), iota((held_queries, LANES), 1) % queries
        for b in range(blocks):
            lse2[r, b] = jnp.sum(
                jnp.where(sub == b * queries + lane, level, 0.0), axis=0, keepdims=True
            )
        to_outer(r, 9, lambda b, r=r: lse2.at[r, b], lse2_in)
        to_outer(r, 8, lambda b, r=r: comb.at[r, b], comb_in)

    square = iota((queries, LANES), 0) == iota((queries, LANES), 1)
    for r in range(2):
        arrived(r, 9, lse2_in)
        level = [
            jnp.sum(jnp.where(square, lse2_in[r, b], 0.0), axis=1, keepdims=True)
            for b in range(blocks)
        ]
        top = functools.reduce(jnp.maximum, level)
        factor = [jnp.exp(v - top) for v in level]
        total = functools.reduce(jnp.add, factor)
        arrived(r, 8, comb_in)
        value = jnp.zeros((queries, half), F32)
        for b in range(blocks):
            value = value + factor[b] * comb_in[r, b].astype(F32)
        retrieved_ref[:, r * half : (r + 1) * half] = (value / total).astype(BF16)
        if r == 0:
            log_total = top + jnp.log(total)
            log_row = jnp.sum(jnp.where(square, log_total, 0.0), axis=0, keepdims=True)
            log_ref[...] = log_row[:, :queries]

    for r in range(2):
        for phase, target in (
            (0, table_in),
            (1, asked_in),
            (2, found_in),
            (3, fsum_in),
            (4, roc_in),
            (5, vec_in),
            (6, part_in),
            (7, lse_in),
            (8, comb_in),
            (9, lse2_in),
        ):
            sent(r, phase, target)


def per_device(queries, passages, list_tiles, probes, fb_probe, fb_row):
    groups, members = lax.axis_size("grp"), lax.axis_size("dev")
    rows, width = passages.shape
    query_rows, probe_count = probes.shape
    fb_count = fb_row.shape[1]
    sizes = (groups, members, rows, query_rows, probe_count, fb_count, width)
    lists, half, slab = groups * members, width // 2, SLOTS * groups
    across = members // (groups // CORES)
    vmem = pl.BlockSpec(memory_space=pltpu.VMEM)
    plane_rows = pltpu.VMEM((2, members, slab, half), BF16)
    plane_int = pltpu.VMEM((2, members, 1, LANES), jnp.int32)
    plane_float = pltpu.VMEM((2, members, 1, LANES), F32)
    outer_rows = pltpu.VMEM((2, groups, query_rows, half), BF16)
    outer_float = pltpu.VMEM((2, groups, 1, LANES), F32)
    retrieved, log_total = pl.pallas_call(
        functools.partial(kernel, sizes),
        out_shape=(
            jax.ShapeDtypeStruct((query_rows, width), BF16),
            jax.ShapeDtypeStruct((1, query_rows), F32),
        ),
        in_specs=[
            vmem,
            vmem,
            vmem,
            vmem,
            pl.BlockSpec(memory_space=pltpu.SMEM),
            pl.BlockSpec(memory_space=pl.ANY),
        ],
        out_specs=(vmem, vmem),
        scratch_shapes=[
            pltpu.VMEM((rows, width), BF16),
            pltpu.VMEM((1, SLOTS * lists), jnp.int32),
            pltpu.VMEM((2, groups, 1, SLOTS * lists), jnp.int32),
            plane_int,
            plane_int,
            plane_int,
            pltpu.VMEM((2, members, slab, groups * query_rows), BF16),
            plane_rows,
            plane_rows,
            outer_rows,
            outer_rows,
            pltpu.VMEM((2, query_rows, half), BF16),
            outer_rows,
            plane_rows,
            plane_rows,
            plane_rows,
            plane_rows,
            plane_float,
            plane_float,
            outer_rows,
            outer_rows,
            outer_float,
            outer_float,
            pltpu.SemaphoreType.DMA,
            pltpu.SemaphoreType.DMA((2, 10)),
            pltpu.SemaphoreType.DMA((2, 10)),
            pltpu.SemaphoreType.DMA((2, across)),
        ],
        compiler_params=pltpu.CompilerParams(
            has_side_effects=True, vmem_limit_bytes=56 * 1024 * 1024
        ),
        name="probe_lists",
    )(queries, probes, fb_probe, fb_row, list_tiles, passages)
    return retrieved, log_total.reshape(query_rows)


def solution(mesh):
    spec = P(("grp", "dev"), None)
    flat = P(("grp", "dev"))
    return jax.shard_map(
        per_device,
        mesh=mesh,
        in_specs=(spec, spec, flat, spec, spec, spec),
        out_specs=(spec, flat),
        check_vma=False,
    )
```

```python
import functools
import math

import jax
import jax.numpy as jnp
from jax import lax
from jax.experimental import pallas as pl
from jax.experimental.pallas import tpu as pltpu
from jax.sharding import PartitionSpec as P

TILE = 128
SLOTS = 2
CORES = 2
LANES = 128
ALPHA_WEIGHT = 1.0
BETA_WEIGHT = 0.75
NEG_FILL = -1e30
F32 = jnp.float32
BF16 = jnp.bfloat16
MESH = pl.DeviceIdType.MESH


def iota(shape, dim):
    return lax.broadcasted_iota(jnp.int32, shape, dim)


def kernel(
    sizes,
    queries_ref,
    probes_ref,
    fb_probe_ref,
    fb_row_ref,
    tiles_ref,
    passages_ref,
    retrieved_ref,
    log_ref,
    held,
    table,
    table_in,
    asked,
    asked_in,
    select,
    spread,
    found,
    found_in,
    fsum,
    fsum_in,
    roc,
    roc_in,
    vec,
    vec_in,
    part,
    part_in,
    lse,
    lse_in,
    comb,
    comb_in,
    lse2,
    lse2_in,
    held_sem,
    send_sem,
    recv_sem,
    vec_sem,
):
    groups, members, rows, queries, probe_count, fb_count, width = sizes
    ring = groups // CORES
    across = members // ring
    lists = groups * members
    half = width // 2
    blocks = groups
    slab = SLOTS * blocks
    plane = members
    chunk = ring * slab
    held_queries = blocks * queries
    slots = plane * slab
    tile_lanes = min(LANES, slots)
    per_tile = tile_lanes // slab

    grp, dev = lax.axis_index("grp"), lax.axis_index("dev")
    z, c = grp // CORES, grp % CORES
    y, x = dev // across, dev % across
    my_b = (grp, y * CORES + c)
    my_o = (y, z)
    my_k = (x * ring + y, x * ring + z)

    def outer_id(r, b):
        if r == 0:
            return (b, dev)
        return (z * CORES + b % CORES, (b // CORES) * across + x)

    def plane_id(r, k):
        far_x, far_o = k // ring, k % ring
        if r == 0:
            return (grp, far_o * across + far_x)
        return (far_o * CORES + c, y * across + far_x)

    def either_way(i, n):
        return jnp.where(i % 2 == 1, (i + 1) // 2, (n - i // 2) % n)

    def send(r, source, target, phase, landed, place):
        pltpu.make_async_remote_copy(
            src_ref=source,
            dst_ref=target,
            send_sem=send_sem.at[r, phase],
            recv_sem=landed,
            device_id=place,
            device_id_type=MESH,
        ).start()

    def to_outer(*items):
        for r in range(2):
            for phase, source, target in items:
                pltpu.make_async_copy(
                    source(r, my_b[r]), target.at[r, my_b[r]], recv_sem.at[r, phase]
                ).start()

        @pl.loop(0, blocks - 1)
        def _(i):
            j = blocks - 1 - i
            step = either_way(j // CORES, ring)
            for r in range(2):
                first = (z, y)[r]
                b = (first + step) % ring * CORES + (c + j) % CORES
                for phase, source, target in items:
                    send(
                        r,
                        source(r, b),
                        target.at[r, my_b[r]],
                        phase,
                        recv_sem.at[r, phase],
                        outer_id(r, b),
                    )

    def to_plane(phase, source, target):
        for r in range(2):
            mine = my_k[r]
            pltpu.make_async_copy(
                source.at[r, mine], target.at[r, mine], recv_sem.at[r, phase]
            ).start()

        @pl.loop(0, plane - 1)
        def _(i):
            j = plane - 1 - i
            step = either_way(j // across, ring)
            for r in range(2):
                k = (x + j) % across * ring + (my_o[r] + step) % ring
                send(
                    r,
                    source.at[r, k],
                    target.at[r, my_k[r]],
                    phase,
                    recv_sem.at[r, phase],
                    plane_id(r, k),
                )

    def to_chunk(t, far_x, *items):
        @pl.when(t == across - 1)
        def _():
            for r in range(2):
                for phase, source, target, landed in items:
                    pltpu.make_async_copy(
                        source.at[r, my_k[r]], target.at[r, my_k[r]], landed(r)
                    ).start()

        @pl.loop(0, ring)
        def _(i):
            step = either_way(ring - 1 - i, ring)

            @pl.when(t + i < across + ring - 2)
            def _():
                for r in range(2):
                    k = far_x * ring + (my_o[r] + step) % ring
                    for phase, source, target, landed in items:
                        send(
                            r,
                            source.at[r, k],
                            target.at[r, my_k[r]],
                            phase,
                            landed(r),
                            plane_id(r, k),
                        )

    def turn_of(t):
        return (across // 2 + either_way(t, across)) % across

    def arrived(r, phase, target):
        pltpu.make_async_copy(target.at[r], target.at[r], recv_sem.at[r, phase]).wait()

    def sent(r, phase, target):
        gone = target.at[r, pl.ds(1, target.shape[1] - 1)]
        pltpu.make_async_copy(gone, gone, send_sem.at[r, phase]).wait()

    barrier = pltpu.get_barrier_semaphore()
    for r in range(2):
        for partners, mine, place in ((blocks, my_b[r], outer_id), (plane, my_k[r], plane_id)):

            @pl.loop(1, partners)
            def _(i, r=r, partners=partners, mine=mine, place=place):
                pl.semaphore_signal(
                    barrier,
                    inc=1,
                    device_id=place(r, (mine + i) % partners),
                    device_id_type=MESH,
                )

    copy_held = pltpu.make_async_copy(passages_ref, held, held_sem)
    copy_held.start()

    probes = probes_ref[...]
    fb_probe, fb_row = fb_probe_ref[...], fb_row_ref[...]
    position = iota((queries, probe_count), 1)
    wanted = jnp.ones((queries, probe_count), jnp.int32)
    for k in range(fb_count):
        wanted = jnp.where(position == fb_probe[:, k : k + 1], fb_row[:, k : k + 1] + 2, wanted)
    list_lane = iota((queries, lists), 1)
    named = jnp.zeros((queries, lists), jnp.int32)
    for j in range(probe_count):
        named = jnp.where(list_lane == probes[:, j : j + 1], wanted[:, j : j + 1], named)
    member = named > 0
    before = jnp.where(iota((queries, queries), 0) > iota((queries, queries), 1), 1.0, 0.0)
    rank = jnp.dot(
        before.astype(BF16),
        jnp.where(member, 1.0, 0.0).astype(BF16),
        preferred_element_type=F32,
    )
    code = (iota((queries, lists), 0) + 1) * 256 + named
    code = jnp.where(member, code, 0)
    for s in range(SLOTS):
        row = jnp.sum(jnp.where(rank == float(s), code, 0), axis=0, keepdims=True)
        table[0:1, s * lists : (s + 1) * lists] = row
    pl.semaphore_wait(barrier, 2 * (blocks - 1 + plane - 1))
    to_outer((0, lambda r, b: table, table_in))

    tiles = plane // per_tile
    list_of = [per_tile * (p % tiles) + p // tiles for p in range(plane)]
    sub_b = iota((blocks, SLOTS * lists), 0)
    sub_p, lane_l = iota((plane, lists), 0), iota((plane, lists), 1)
    far_k = per_tile * (sub_p % tiles) + sub_p // tiles
    lane_slab = iota((tiles, LANES), 1)
    contract_last = (((1,), (1,)), ((), ()))
    slot_codes, list_hots = [], []
    for r in range(2):
        arrived(r, 0, table_in)
        all_codes = jnp.zeros((blocks, SLOTS * lists), jnp.int32)
        for b in range(blocks):
            all_codes = jnp.where(sub_b == b, table_in[r, b], all_codes)
        all_codes = jnp.concatenate(
            [all_codes[:, s * lists : (s + 1) * lists] for s in range(SLOTS)], axis=0
        )
        far_grp, far_dev = plane_id(r, far_k)
        list_hot = jnp.where(lane_l == far_grp * members + far_dev, 1.0, 0.0).astype(BF16)
        want = (all_codes & 255).astype(F32).astype(BF16)
        want_rows = lax.dot_general(
            list_hot,
            jnp.concatenate([want] * (LANES // slab), axis=0),
            contract_last,
            preferred_element_type=F32,
        )
        for p, k in enumerate(list_of):
            asked[r, k] = want_rows[p : p + 1]
        slot_codes.append((all_codes >> 8).astype(F32).astype(BF16))
        list_hots.append(list_hot)
    to_plane(1, asked, asked_in)

    first_of = (iota((slab, plane), 0) % blocks * queries).astype(F32)
    query_lane = iota((slab, held_queries), 1).astype(F32)
    sub_q = iota((held_queries, tile_lanes), 0).astype(F32)
    for r in range(2):
        column = lax.dot_general(
            slot_codes[r], list_hots[r], contract_last, preferred_element_type=F32
        )
        column = jnp.where(column > 0.0, first_of + column - 1.0, -1.0)
        for p, k in enumerate(list_of):
            select[r, k] = jnp.where(query_lane == column[:, p : p + 1], 1.0, 0.0).astype(BF16)
        rows_of = lax.dot_general(
            list_hots[r],
            jnp.concatenate([slot_codes[r]] * (LANES // slab), axis=0),
            contract_last,
            preferred_element_type=F32,
        )
        joined = rows_of[:tiles]
        for i in range(1, per_tile):
            joined = jnp.where(
                lane_slab // slab == i, rows_of[i * tiles : (i + 1) * tiles], joined
            )
        joined = jnp.where(
            joined > 0.0, (lane_slab % blocks * queries).astype(F32) + joined - 1.0, -1.0
        )
        for j in range(tiles):
            spread[r, :, j * tile_lanes : (j + 1) * tile_lanes] = jnp.where(
                sub_q == joined[j : j + 1, :tile_lanes], 1.0, 0.0
            ).astype(BF16)

    tile_source = iota((1, tile_lanes), 1) // slab
    copy_held.wait()

    def lane_tile(ref, r, j):
        row = ref[r, per_tile * j][:, :tile_lanes]
        for i in range(1, per_tile):
            row = jnp.where(tile_source == i, ref[r, per_tile * j + i][:, :tile_lanes], row)
        return row

    for r in range(2):
        arrived(r, 1, asked_in)
        first = held[0:TILE, r * half : (r + 1) * half]
        sub_row = (iota((TILE, tile_lanes), 0) + 2).astype(F32)
        for j in range(tiles):
            row = lane_tile(asked_in, r, j)
            hot = jnp.where(sub_row == row, 1.0, 0.0).astype(BF16)
            picked = lax.dot_general(
                hot, first, (((0,), (0,)), ((), ())), preferred_element_type=F32
            ).astype(BF16)
            found[r, per_tile * j : per_tile * (j + 1)] = picked.reshape(per_tile, slab, half)
    to_plane(2, found, found_in)

    for r in range(2):
        arrived(r, 2, found_in)
        total = jnp.dot(spread[r], found_in[r].reshape(slots, half), preferred_element_type=F32)
        fsum[r] = total.astype(BF16).reshape(blocks, queries, half)
    to_outer((3, lambda r, b: fsum.at[r, b], fsum_in))

    for r in range(2):
        arrived(r, 3, fsum_in)
        total = jnp.zeros((queries, half), F32)
        for b in range(blocks):
            total = total + fsum_in[r, b].astype(F32)
        own = queries_ref[:, r * half : (r + 1) * half].astype(F32)
        roc[r] = (ALPHA_WEIGHT * own + BETA_WEIGHT * (total / fb_count)).astype(BF16)
    to_outer((4, lambda r, b: roc.at[r], roc_in))

    for r in range(2):
        arrived(r, 4, roc_in)

    @pl.loop(0, across)
    def _(t):
        far_x = (x + turn_of(t)) % across
        there = pl.ds(far_x * ring, ring)
        for r in range(2):
            picked = jnp.dot(
                select[r, there].reshape(chunk, held_queries),
                roc_in[r].reshape(held_queries, half),
                preferred_element_type=F32,
            )
            vec[r, there] = picked.astype(BF16).reshape(ring, slab, half)
        to_chunk(t, far_x, (5, vec, vec_in, lambda r: vec_sem.at[r, x]))

    scale = 3.0 / math.sqrt(width)
    live = tiles_ref[0] * TILE
    bits = slab // 2
    turn = iota((slab, LANES), 0) == iota((slab, LANES), 1) % slab

    def swapped(index):
        o, s, low = index // slab, (index % slab) // bits, index % bits
        return (low // CORES) * slab + s * bits + o * CORES + low % CORES

    swap = jnp.where(
        iota((chunk, chunk), 0) == swapped(iota((chunk, chunk), 1)), 1.0, 0.0
    ).astype(BF16)

    @pl.loop(0, across)
    def _(t):
        far_x = (x + across - turn_of(t)) % across
        there = pl.ds(far_x * ring, ring)
        for r in range(2):
            landed = vec_in.at[r, there]
            pltpu.make_async_copy(landed, landed, vec_sem.at[r, far_x]).wait()
        first = vec_in[0, there].reshape(chunk, half)
        second = jnp.dot(
            swap, vec_in[1, there].reshape(chunk, half), preferred_element_type=F32
        ).astype(BF16)
        scores = lax.dot_general(first, held[:, :half], contract_last, preferred_element_type=F32)
        scores = scores + lax.dot_general(
            second, held[:, half:], contract_last, preferred_element_type=F32
        )
        scores = jnp.where(iota((chunk, rows), 1) < live, scores * scale, NEG_FILL)
        peak = jnp.max(scores, axis=1, keepdims=True)
        weights = jnp.exp(scores - peak)
        mass = jnp.sum(weights, axis=1, keepdims=True)
        value = jnp.dot(weights.astype(BF16), held[...], preferred_element_type=F32)
        value = (value / mass).astype(BF16)
        level = peak + jnp.log(mass)
        part[0, there] = value[:, :half].reshape(ring, slab, half)
        part[1, there] = (
            jnp.dot(swap, value[:, half:], preferred_element_type=F32)
            .astype(BF16)
            .reshape(ring, slab, half)
        )
        sub, lane = iota((chunk, LANES), 0), iota((chunk, LANES), 1) % slab
        for o in range(ring):
            near = level[o * slab : (o + 1) * slab]
            row = jnp.sum(jnp.where(turn, near, 0.0), axis=0, keepdims=True)
            lse[0, far_x * ring + o] = row
            place = swapped(o * slab + lane)
            row = jnp.sum(jnp.where(sub == place, level, 0.0), axis=0, keepdims=True)
            lse[1, far_x * ring + o] = row
        to_chunk(
            t,
            far_x,
            (7, lse, lse_in, lambda r: recv_sem.at[r, 7]),
            (6, part, part_in, lambda r: recv_sem.at[r, 6]),
        )

    square = iota((queries, LANES), 0) == iota((queries, LANES), 1)
    for r in range(2):
        arrived(r, 7, lse_in)
        levels = jnp.concatenate([lane_tile(lse_in, r, j) for j in range(tiles)], axis=1)
        mask = spread[r].astype(F32) > 0.0
        levels = jnp.where(mask, levels, NEG_FILL)
        top = jnp.max(levels, axis=1, keepdims=True)
        weights = jnp.where(mask, jnp.exp(levels - top), 0.0)
        total = jnp.sum(weights, axis=1, keepdims=True)
        high = weights.astype(BF16)
        low = (weights - high.astype(F32)).astype(BF16)
        arrived(r, 6, part_in)
        parts = part_in[r].reshape(slots, half)
        value = jnp.dot(high, parts, preferred_element_type=F32)
        value = value + jnp.dot(low, parts, preferred_element_type=F32)
        some = total > 0.0
        total = jnp.where(some, total, 1.0)
        comb[r] = (value / total).astype(BF16).reshape(blocks, queries, half)
        level = jnp.where(some, top + jnp.log(total), NEG_FILL)
        for b in range(blocks):
            near = level[b * queries : (b + 1) * queries]
            lse2[r, b] = jnp.sum(jnp.where(square, near, 0.0), axis=0, keepdims=True)
    to_outer((9, lambda r, b: lse2.at[r, b], lse2_in), (8, lambda r, b: comb.at[r, b], comb_in))

    for r in range(2):
        arrived(r, 9, lse2_in)
        level = [
            jnp.sum(jnp.where(square, lse2_in[r, b], 0.0), axis=1, keepdims=True)
            for b in range(blocks)
        ]
        top = functools.reduce(jnp.maximum, level)
        factor = [jnp.exp(v - top) for v in level]
        total = functools.reduce(jnp.add, factor)
        arrived(r, 8, comb_in)
        value = jnp.zeros((queries, half), F32)
        for b in range(blocks):
            value = value + factor[b] * comb_in[r, b].astype(F32)
        retrieved_ref[:, r * half : (r + 1) * half] = (value / total).astype(BF16)
        if r == 0:
            log_total = top + jnp.log(total)
            log_row = jnp.sum(jnp.where(square, log_total, 0.0), axis=0, keepdims=True)
            log_ref[...] = log_row[:, :queries]

    for r in range(2):
        for phase, target in (
            (0, table_in),
            (1, asked_in),
            (2, found_in),
            (3, fsum_in),
            (4, roc_in),
            (5, vec_in),
            (6, part_in),
            (7, lse_in),
            (8, comb_in),
            (9, lse2_in),
        ):
            sent(r, phase, target)


def per_device(queries, passages, list_tiles, probes, fb_probe, fb_row):
    groups, members = lax.axis_size("grp"), lax.axis_size("dev")
    rows, width = passages.shape
    query_rows, probe_count = probes.shape
    fb_count = fb_row.shape[1]
    sizes = (groups, members, rows, query_rows, probe_count, fb_count, width)
    lists, half, slab = groups * members, width // 2, SLOTS * groups
    across = members // (groups // CORES)
    slots = members * slab
    tile_lanes = min(LANES, slots)
    vmem = pl.BlockSpec(memory_space=pltpu.VMEM)
    plane_rows = pltpu.VMEM((2, members, slab, half), BF16)
    plane_float = pltpu.VMEM((2, members, 1, LANES), F32)
    outer_rows = pltpu.VMEM((2, groups, query_rows, half), BF16)
    outer_float = pltpu.VMEM((2, groups, 1, LANES), F32)
    retrieved, log_total = pl.pallas_call(
        functools.partial(kernel, sizes),
        out_shape=(
            jax.ShapeDtypeStruct((query_rows, width), BF16),
            jax.ShapeDtypeStruct((1, query_rows), F32),
        ),
        in_specs=[
            vmem,
            vmem,
            vmem,
            vmem,
            pl.BlockSpec(memory_space=pltpu.SMEM),
            pl.BlockSpec(memory_space=pl.ANY),
        ],
        out_specs=(vmem, vmem),
        scratch_shapes=[
            pltpu.VMEM((rows, width), BF16),
            pltpu.VMEM((1, SLOTS * lists), jnp.int32),
            pltpu.VMEM((2, groups, 1, SLOTS * lists), jnp.int32),
            plane_float,
            plane_float,
            pltpu.VMEM((2, members, slab, groups * query_rows), BF16),
            pltpu.VMEM((2, groups * query_rows, slots), BF16),
            plane_rows,
            plane_rows,
            outer_rows,
            outer_rows,
            pltpu.VMEM((2, query_rows, half), BF16),
            outer_rows,
            plane_rows,
            plane_rows,
            plane_rows,
            plane_rows,
            plane_float,
            plane_float,
            outer_rows,
            outer_rows,
            outer_float,
            outer_float,
            pltpu.SemaphoreType.DMA,
            pltpu.SemaphoreType.DMA((2, 10)),
            pltpu.SemaphoreType.DMA((2, 10)),
            pltpu.SemaphoreType.DMA((2, across)),
        ],
        compiler_params=pltpu.CompilerParams(
            collective_id=0, has_side_effects=True, vmem_limit_bytes=56 * 1024 * 1024
        ),
        name="probe_lists",
    )(queries, probes, fb_probe, fb_row, list_tiles, passages)
    return retrieved, log_total.reshape(query_rows)


def solution(mesh):
    spec = P(("grp", "dev"), None)
    flat = P(("grp", "dev"))
    return jax.shard_map(
        per_device,
        mesh=mesh,
        in_specs=(spec, spec, flat, spec, spec, spec),
        out_specs=(spec, flat),
        check_vma=False,
    )
```

```python
import functools
import math

import jax
import jax.numpy as jnp
from jax import lax
from jax.experimental import pallas as pl
from jax.experimental.pallas import tpu as pltpu
from jax.sharding import PartitionSpec as P

TILE = 128
SLOTS = 2
CORES = 2
LANES = 128
ALPHA_WEIGHT = 1.0
BETA_WEIGHT = 0.75
NEG_FILL = -1e30
F32 = jnp.float32
BF16 = jnp.bfloat16
MESH = pl.DeviceIdType.MESH


def iota(shape, dim):
    return lax.broadcasted_iota(jnp.int32, shape, dim)


def kernel(
    sizes,
    queries_ref,
    probes_ref,
    fb_probe_ref,
    fb_row_ref,
    tiles_ref,
    passages_ref,
    retrieved_ref,
    log_ref,
    held,
    table,
    table_in,
    asked,
    asked_in,
    select,
    spread,
    found,
    found_in,
    fsum,
    fsum_in,
    roc,
    roc_in,
    vec,
    vec_in,
    part,
    part_in,
    lse,
    lse_in,
    comb,
    comb_in,
    lse2,
    lse2_in,
    held_sem,
    send_sem,
    recv_sem,
    vec_sem,
    vec_sent_sem,
):
    groups, members, rows, queries, probe_count, fb_count, width = sizes
    ring = groups // CORES
    across = members // ring
    lists = groups * members
    half = width // 2
    blocks = groups
    slab = SLOTS * blocks
    plane = members
    chunk = ring * slab
    held_queries = blocks * queries
    slots = plane * slab
    tile_lanes = min(LANES, slots)
    per_tile = tile_lanes // slab

    grp, dev = lax.axis_index("grp"), lax.axis_index("dev")
    z, c = grp // CORES, grp % CORES
    y, x = dev // across, dev % across
    my_b = (grp, y * CORES + c)
    my_k = (x * ring + y, x * ring + z)

    def wrap(index, n):
        return jnp.where(index >= n, index - n, index)

    steps = sorted(range(ring), key=lambda step: -min(step, ring - step))
    far_y = [wrap(y + step, ring) for step in steps]
    far_z = [wrap(z + step, ring) for step in steps]
    dev_y = [v * across for v in far_y]
    grp_z = [v * CORES for v in far_z]
    row_y, column_z = y * across, z * CORES

    def plane_place(r, n, far_x):
        if r == 0:
            return far_x * ring + far_y[n], (grp, dev_y[n] + far_x)
        return far_x * ring + far_z[n], (grp_z[n] + c, row_y + far_x)

    def outer_place(r, n, far_c):
        if r == 0:
            return grp_z[n] + far_c, (grp_z[n] + far_c, dev)
        return far_y[n] * CORES + far_c, (column_z + far_c, dev_y[n] + x)

    def far_x_of(t):
        if across == 4:
            return jnp.where(t == 0, 0, jnp.where(t == 1, 2, jnp.where(t == 2, 3, 1)))
        return t

    def each_plane(t, far_x, act):
        for n in range(ring):
            for r in range(2):
                k, place = plane_place(r, n, far_x)
                if n < ring - 1:
                    act(r, k, place)
                else:
                    pl.when(t > 0)(functools.partial(act, r, k, place))

    def each_outer(act):
        @pl.loop(0, CORES)
        def _(t):
            far_c = jnp.where(t == 0, 1 - c, c)
            for n in range(ring):
                for r in range(2):
                    b, place = outer_place(r, n, far_c)
                    if n < ring - 1:
                        act(r, b, place)
                    else:
                        pl.when(t < CORES - 1)(functools.partial(act, r, b, place))

    def send(r, source, target, left, landed, place):
        pltpu.make_async_remote_copy(
            src_ref=source,
            dst_ref=target,
            send_sem=left,
            recv_sem=landed,
            device_id=place,
            device_id_type=MESH,
        ).start()

    def to_outer(*items):
        for r in range(2):
            for phase, source, target in items:
                pltpu.make_async_copy(
                    source(r, my_b[r]), target.at[r, my_b[r]], recv_sem.at[r, phase]
                ).start()

        def act(r, b, place):
            for phase, source, target in items:
                send(
                    r,
                    source(r, b),
                    target.at[r, my_b[r]],
                    send_sem.at[r, phase],
                    recv_sem.at[r, phase],
                    place,
                )

        each_outer(act)

    def to_chunk(t, far_x, *items):
        @pl.when(t == 0)
        def _():
            for r in range(2):
                for left, source, target, landed in items:
                    pltpu.make_async_copy(
                        source.at[r, my_k[r]], target.at[r, my_k[r]], landed(r)
                    ).start()

        def act(r, k, place):
            for left, source, target, landed in items:
                send(r, source.at[r, k], target.at[r, my_k[r]], left(r), landed(r), place)

        each_plane(t, far_x, act)

    def both_ends(phase, source, target):
        return (
            lambda r: send_sem.at[r, phase],
            source,
            target,
            lambda r: recv_sem.at[r, phase],
        )

    def chunk_sent(t):
        for r in range(2):
            gone = vec.at[r, pl.ds(0, ring - 1 if t == 0 else ring)]
            pltpu.make_async_copy(gone, gone, vec_sent_sem.at[r, t]).wait()

    def to_plane(phase, source, target):
        @pl.loop(0, across)
        def _(t):
            far_x = wrap(x + far_x_of(t), across)
            to_chunk(t, far_x, both_ends(phase, source, target))

    def arrived(r, phase, target):
        pltpu.make_async_copy(target.at[r], target.at[r], recv_sem.at[r, phase]).wait()

    def sent(r, phase, target):
        gone = target.at[r, pl.ds(1, target.shape[1] - 1)]
        pltpu.make_async_copy(gone, gone, send_sem.at[r, phase]).wait()

    barrier = pltpu.get_barrier_semaphore()

    def greet(r, index, place):
        pl.semaphore_signal(barrier, inc=1, device_id=place, device_id_type=MESH)

    each_outer(greet)

    @pl.loop(0, across)
    def _(t):
        each_plane(t, wrap(x + far_x_of(t), across), greet)

    copy_held = pltpu.make_async_copy(passages_ref, held, held_sem)
    copy_held.start()

    probes = probes_ref[...]
    fb_probe, fb_row = fb_probe_ref[...], fb_row_ref[...]
    position = iota((queries, probe_count), 1)
    wanted = jnp.ones((queries, probe_count), jnp.int32)
    for k in range(fb_count):
        wanted = jnp.where(position == fb_probe[:, k : k + 1], fb_row[:, k : k + 1] + 2, wanted)
    list_lane = iota((queries, lists), 1)
    named = jnp.zeros((queries, lists), jnp.int32)
    for j in range(probe_count):
        named = jnp.where(list_lane == probes[:, j : j + 1], wanted[:, j : j + 1], named)
    member = named > 0
    before = jnp.where(iota((queries, queries), 0) > iota((queries, queries), 1), 1.0, 0.0)
    rank = jnp.dot(
        before.astype(BF16),
        jnp.where(member, 1.0, 0.0).astype(BF16),
        preferred_element_type=F32,
    )
    code = (iota((queries, lists), 0) + 1) * 256 + named
    code = jnp.where(member, code, 0)
    for s in range(SLOTS):
        row = jnp.sum(jnp.where(rank == float(s), code, 0), axis=0, keepdims=True)
        table[0:1, s * lists : (s + 1) * lists] = row
    pl.semaphore_wait(barrier, 2 * (blocks - 1 + plane - 1))
    to_outer((0, lambda r, b: table, table_in))

    tiles = plane // per_tile
    list_of = [per_tile * (p % tiles) + p // tiles for p in range(plane)]
    sub_b = iota((blocks, SLOTS * lists), 0)
    sub_p, lane_l = iota((plane, lists), 0), iota((plane, lists), 1)
    far_k = per_tile * (sub_p % tiles) + sub_p // tiles
    lane_slab = iota((tiles, LANES), 1)
    contract_last = (((1,), (1,)), ((), ()))
    slot_codes, list_hots = [], []
    for r in range(2):
        arrived(r, 0, table_in)
        all_codes = jnp.zeros((blocks, SLOTS * lists), jnp.int32)
        for b in range(blocks):
            all_codes = jnp.where(sub_b == b, table_in[r, b], all_codes)
        all_codes = jnp.concatenate(
            [all_codes[:, s * lists : (s + 1) * lists] for s in range(SLOTS)], axis=0
        )
        far_o, far_column = far_k % ring, far_k // ring
        if r == 0:
            far_list = grp * members + far_o * across + far_column
        else:
            far_list = (far_o * CORES + c) * members + row_y + far_column
        list_hot = jnp.where(lane_l == far_list, 1.0, 0.0).astype(BF16)
        want = (all_codes & 255).astype(F32).astype(BF16)
        want_rows = lax.dot_general(
            list_hot,
            jnp.concatenate([want] * (LANES // slab), axis=0),
            contract_last,
            preferred_element_type=F32,
        )
        for p, k in enumerate(list_of):
            asked[r, k] = want_rows[p : p + 1]
        slot_codes.append((all_codes >> 8).astype(F32).astype(BF16))
        list_hots.append(list_hot)
    to_plane(1, asked, asked_in)

    first_of = (iota((slab, plane), 0) % blocks * queries).astype(F32)
    query_lane = iota((slab, held_queries), 1).astype(F32)
    sub_q = iota((held_queries, tile_lanes), 0).astype(F32)
    for r in range(2):
        column = lax.dot_general(
            slot_codes[r], list_hots[r], contract_last, preferred_element_type=F32
        )
        column = jnp.where(column > 0.0, first_of + column - 1.0, -1.0)
        for p, k in enumerate(list_of):
            select[r, k] = jnp.where(query_lane == column[:, p : p + 1], 1.0, 0.0).astype(BF16)
        rows_of = lax.dot_general(
            list_hots[r],
            jnp.concatenate([slot_codes[r]] * (LANES // slab), axis=0),
            contract_last,
            preferred_element_type=F32,
        )
        joined = rows_of[:tiles]
        for i in range(1, per_tile):
            joined = jnp.where(
                lane_slab // slab == i, rows_of[i * tiles : (i + 1) * tiles], joined
            )
        joined = jnp.where(
            joined > 0.0, (lane_slab % blocks * queries).astype(F32) + joined - 1.0, -1.0
        )
        for j in range(tiles):
            spread[r, :, j * tile_lanes : (j + 1) * tile_lanes] = jnp.where(
                sub_q == joined[j : j + 1, :tile_lanes], 1.0, 0.0
            ).astype(BF16)

    tile_source = iota((1, tile_lanes), 1) // slab
    copy_held.wait()

    def lane_tile(ref, r, j):
        row = ref[r, per_tile * j][:, :tile_lanes]
        for i in range(1, per_tile):
            row = jnp.where(tile_source == i, ref[r, per_tile * j + i][:, :tile_lanes], row)
        return row

    for r in range(2):
        arrived(r, 1, asked_in)
        first = held[0:TILE, r * half : (r + 1) * half]
        sub_row = (iota((TILE, tile_lanes), 0) + 2).astype(F32)
        for j in range(tiles):
            row = lane_tile(asked_in, r, j)
            hot = jnp.where(sub_row == row, 1.0, 0.0).astype(BF16)
            picked = lax.dot_general(
                hot, first, (((0,), (0,)), ((), ())), preferred_element_type=F32
            ).astype(BF16)
            found[r, per_tile * j : per_tile * (j + 1)] = picked.reshape(per_tile, slab, half)
    to_plane(2, found, found_in)

    for r in range(2):
        arrived(r, 2, found_in)
        total = jnp.dot(spread[r], found_in[r].reshape(slots, half), preferred_element_type=F32)
        fsum[r] = total.astype(BF16).reshape(blocks, queries, half)
    to_outer((3, lambda r, b: fsum.at[r, b], fsum_in))

    for r in range(2):
        arrived(r, 3, fsum_in)
        total = jnp.zeros((queries, half), F32)
        for b in range(blocks):
            total = total + fsum_in[r, b].astype(F32)
        own = queries_ref[:, r * half : (r + 1) * half].astype(F32)
        roc[r] = (ALPHA_WEIGHT * own + BETA_WEIGHT * (total / fb_count)).astype(BF16)
    to_outer((4, lambda r, b: roc.at[r], roc_in))

    for r in range(2):
        arrived(r, 4, roc_in)

    @pl.loop(0, across)
    def _(t):
        far_x = wrap(x + far_x_of(t), across)
        there = pl.ds(far_x * ring, ring)
        for r in range(2):
            picked = jnp.dot(
                select[r, there].reshape(chunk, held_queries),
                roc_in[r].reshape(held_queries, half),
                preferred_element_type=F32,
            )
            vec[r, there] = picked.astype(BF16).reshape(ring, slab, half)
        for late in range(2, across):
            pl.when(t == late)(functools.partial(chunk_sent, late - 2))
        to_chunk(
            t,
            far_x,
            (lambda r: vec_sent_sem.at[r, t], vec, vec_in, lambda r: vec_sem.at[r, x]),
        )

    scale = 3.0 / math.sqrt(width)
    live = tiles_ref[0] * TILE
    bits = slab // 2
    turn = iota((slab, LANES), 0) == iota((slab, LANES), 1) % slab
    term_lane = iota((chunk, LANES), 1)

    def swapped(index):
        o, s, low = index // slab, (index % slab) // bits, index % bits
        return (low // CORES) * slab + s * bits + o * CORES + low % CORES

    swap = jnp.where(
        iota((chunk, chunk), 0) == swapped(iota((chunk, chunk), 1)), 1.0, 0.0
    ).astype(BF16)

    @pl.loop(0, across)
    def _(t):
        far_x = wrap(x + wrap(across - far_x_of(t), across), across)
        there = pl.ds(far_x * ring, ring)
        for r in range(2):
            landed = vec_in.at[r, there]
            pltpu.make_async_copy(landed, landed, vec_sem.at[r, far_x]).wait()
        first = vec_in[0, there].reshape(chunk, half)
        second = jnp.dot(
            swap, vec_in[1, there].reshape(chunk, half), preferred_element_type=F32
        ).astype(BF16)
        scores = lax.dot_general(
            jnp.concatenate([first, second], axis=1),
            held[...],
            contract_last,
            preferred_element_type=F32,
        )
        scores = jnp.where(iota((chunk, rows), 1) < live, scores * scale, NEG_FILL)
        peak = jnp.max(scores, axis=1, keepdims=True)
        weights = jnp.exp(scores - peak)
        mass = jnp.sum(weights, axis=1, keepdims=True)
        value = jnp.dot(weights.astype(BF16), held[...], preferred_element_type=F32)
        value = (value / mass).astype(BF16)
        level = peak + jnp.log(mass)
        part[0, there] = value[:, :half].reshape(ring, slab, half)
        rest, terms = level, jnp.zeros((chunk, LANES), F32)
        for i in range(3):
            term = rest.astype(BF16).astype(F32)
            terms = jnp.where(term_lane == i, term, terms)
            rest = rest - term
        moved = jnp.dot(
            swap,
            jnp.concatenate([value[:, half:], terms.astype(BF16)], axis=1),
            preferred_element_type=F32,
        )
        part[1, there] = moved[:, :half].astype(BF16).reshape(ring, slab, half)
        levels = (level, jnp.sum(moved[:, half:], axis=1, keepdims=True))
        for o in range(ring):
            for r in range(2):
                near = levels[r][o * slab : (o + 1) * slab]
                row = jnp.sum(jnp.where(turn, near, 0.0), axis=0, keepdims=True)
                lse[r, far_x * ring + o] = row
        to_chunk(
            t,
            far_x,
            both_ends(7, lse, lse_in),
            both_ends(6, part, part_in),
        )

    square = iota((queries, LANES), 0) == iota((queries, LANES), 1)
    for r in range(2):
        arrived(r, 7, lse_in)
        levels = jnp.concatenate([lane_tile(lse_in, r, j) for j in range(tiles)], axis=1)
        mask = spread[r].astype(F32) > 0.0
        levels = jnp.where(mask, levels, NEG_FILL)
        top = jnp.max(levels, axis=1, keepdims=True)
        weights = jnp.where(mask, jnp.exp(levels - top), 0.0)
        total = jnp.sum(weights, axis=1, keepdims=True)
        high = weights.astype(BF16)
        low = (weights - high.astype(F32)).astype(BF16)
        arrived(r, 6, part_in)
        parts = part_in[r].reshape(slots, half)
        value = jnp.dot(high, parts, preferred_element_type=F32)
        value = value + jnp.dot(low, parts, preferred_element_type=F32)
        some = total > 0.0
        total = jnp.where(some, total, 1.0)
        comb[r] = (value / total).astype(BF16).reshape(blocks, queries, half)
        level = jnp.where(some, top + jnp.log(total), NEG_FILL)
        for b in range(blocks):
            near = level[b * queries : (b + 1) * queries]
            lse2[r, b] = jnp.sum(jnp.where(square, near, 0.0), axis=0, keepdims=True)
    to_outer((9, lambda r, b: lse2.at[r, b], lse2_in), (8, lambda r, b: comb.at[r, b], comb_in))

    for r in range(2):
        arrived(r, 9, lse2_in)
        level = [
            jnp.sum(jnp.where(square, lse2_in[r, b], 0.0), axis=1, keepdims=True)
            for b in range(blocks)
        ]
        top = functools.reduce(jnp.maximum, level)
        factor = [jnp.exp(v - top) for v in level]
        total = functools.reduce(jnp.add, factor)
        arrived(r, 8, comb_in)
        value = jnp.zeros((queries, half), F32)
        for b in range(blocks):
            value = value + factor[b] * comb_in[r, b].astype(F32)
        retrieved_ref[:, r * half : (r + 1) * half] = (value / total).astype(BF16)
        if r == 0:
            log_total = top + jnp.log(total)
            log_row = jnp.sum(jnp.where(square, log_total, 0.0), axis=0, keepdims=True)
            log_ref[...] = log_row[:, :queries]

    for t in range(max(0, across - 2), across):
        chunk_sent(t)
    for r in range(2):
        for phase, target in (
            (0, table_in),
            (1, asked_in),
            (2, found_in),
            (3, fsum_in),
            (4, roc_in),
            (6, part_in),
            (7, lse_in),
            (8, comb_in),
            (9, lse2_in),
        ):
            sent(r, phase, target)


def per_device(queries, passages, list_tiles, probes, fb_probe, fb_row):
    groups, members = lax.axis_size("grp"), lax.axis_size("dev")
    rows, width = passages.shape
    query_rows, probe_count = probes.shape
    fb_count = fb_row.shape[1]
    sizes = (groups, members, rows, query_rows, probe_count, fb_count, width)
    lists, half, slab = groups * members, width // 2, SLOTS * groups
    across = members // (groups // CORES)
    slots = members * slab
    tile_lanes = min(LANES, slots)
    vmem = pl.BlockSpec(memory_space=pltpu.VMEM)
    plane_rows = pltpu.VMEM((2, members, slab, half), BF16)
    plane_float = pltpu.VMEM((2, members, 1, LANES), F32)
    outer_rows = pltpu.VMEM((2, groups, query_rows, half), BF16)
    outer_float = pltpu.VMEM((2, groups, 1, LANES), F32)
    retrieved, log_total = pl.pallas_call(
        functools.partial(kernel, sizes),
        out_shape=(
            jax.ShapeDtypeStruct((query_rows, width), BF16),
            jax.ShapeDtypeStruct((1, query_rows), F32),
        ),
        in_specs=[
            vmem,
            vmem,
            vmem,
            vmem,
            pl.BlockSpec(memory_space=pltpu.SMEM),
            pl.BlockSpec(memory_space=pl.ANY),
        ],
        out_specs=(vmem, vmem),
        scratch_shapes=[
            pltpu.VMEM((rows, width), BF16),
            pltpu.VMEM((1, SLOTS * lists), jnp.int32),
            pltpu.VMEM((2, groups, 1, SLOTS * lists), jnp.int32),
            plane_float,
            plane_float,
            pltpu.VMEM((2, members, slab, groups * query_rows), BF16),
            pltpu.VMEM((2, groups * query_rows, slots), BF16),
            plane_rows,
            plane_rows,
            outer_rows,
            outer_rows,
            pltpu.VMEM((2, query_rows, half), BF16),
            outer_rows,
            plane_rows,
            plane_rows,
            plane_rows,
            plane_rows,
            plane_float,
            plane_float,
            outer_rows,
            outer_rows,
            outer_float,
            outer_float,
            pltpu.SemaphoreType.DMA,
            pltpu.SemaphoreType.DMA((2, 10)),
            pltpu.SemaphoreType.DMA((2, 10)),
            pltpu.SemaphoreType.DMA((2, across)),
            pltpu.SemaphoreType.DMA((2, across)),
        ],
        compiler_params=pltpu.CompilerParams(
            collective_id=0, has_side_effects=True, vmem_limit_bytes=56 * 1024 * 1024
        ),
        name="probe_lists",
    )(queries, probes, fb_probe, fb_row, list_tiles, passages)
    return retrieved, log_total.reshape(query_rows)


def solution(mesh):
    spec = P(("grp", "dev"), None)
    flat = P(("grp", "dev"))
    return jax.shard_map(
        per_device,
        mesh=mesh,
        in_specs=(spec, spec, flat, spec, spec, spec),
        out_specs=(spec, flat),
        check_vma=False,
    )
```

```python
import functools
import math

import jax
import jax.numpy as jnp
from jax import lax
from jax.experimental import pallas as pl
from jax.experimental.pallas import tpu as pltpu
from jax.sharding import PartitionSpec as P

TILE = 128
SLOTS = 2
CORES = 2
LANES = 128
ALPHA_WEIGHT = 1.0
BETA_WEIGHT = 0.75
NEG_FILL = -1e30
F32 = jnp.float32
BF16 = jnp.bfloat16
MESH = pl.DeviceIdType.MESH


def iota(shape, dim):
    return lax.broadcasted_iota(jnp.int32, shape, dim)


def kernel(
    sizes,
    queries_ref,
    probes_ref,
    fb_probe_ref,
    fb_row_ref,
    tiles_ref,
    passages_ref,
    retrieved_ref,
    log_ref,
    held,
    table,
    table_in,
    asked,
    asked_in,
    select,
    spread,
    found,
    found_in,
    fsum,
    fsum_in,
    roc,
    roc_in,
    vec,
    vec_in,
    part,
    part_in,
    lse,
    lse_in,
    comb,
    comb_in,
    lse2,
    lse2_in,
    held_sem,
    send_sem,
    recv_sem,
    vec_sem,
):
    groups, members, rows, queries, probe_count, fb_count, width = sizes
    ring = groups // CORES
    across = members // ring
    lists = groups * members
    half = width // 2
    blocks = groups
    slab = SLOTS * blocks
    plane = members
    chunk = ring * slab
    held_queries = blocks * queries
    slots = plane * slab
    tile_lanes = min(LANES, slots)
    per_tile = tile_lanes // slab

    grp, dev = lax.axis_index("grp"), lax.axis_index("dev")
    z, c = grp // CORES, grp % CORES
    y, x = dev // across, dev % across
    my_b = (grp, y * CORES + c)
    my_k = (x * ring + y, x * ring + z)

    def wrap(index, n):
        return jnp.where(index >= n, index - n, index)

    steps = sorted(range(ring), key=lambda step: -min(step, ring - step))
    far_y = [wrap(y + step, ring) for step in steps]
    far_z = [wrap(z + step, ring) for step in steps]
    dev_y = [v * across for v in far_y]
    grp_z = [v * CORES for v in far_z]
    row_y, column_z = y * across, z * CORES

    def plane_place(r, n, far_x):
        if r == 0:
            return far_x * ring + far_y[n], (grp, dev_y[n] + far_x)
        return far_x * ring + far_z[n], (grp_z[n] + c, row_y + far_x)

    def outer_place(r, n, far_c):
        if r == 0:
            return grp_z[n] + far_c, (grp_z[n] + far_c, dev)
        return far_y[n] * CORES + far_c, (column_z + far_c, dev_y[n] + x)

    def far_x_of(t):
        if across == 4:
            return jnp.where(t == 0, 0, jnp.where(t == 1, 2, jnp.where(t == 2, 3, 1)))
        return t

    def each_plane(t, far_x, act):
        for n in range(ring):
            for r in range(2):
                k, place = plane_place(r, n, far_x)
                if n < ring - 1:
                    act(r, k, place)
                else:
                    pl.when(t > 0)(functools.partial(act, r, k, place))

    def each_outer(act):
        @pl.loop(0, CORES)
        def _(t):
            far_c = jnp.where(t == 0, 1 - c, c)
            for n in range(ring):
                for r in range(2):
                    b, place = outer_place(r, n, far_c)
                    if n < ring - 1:
                        act(r, b, place)
                    else:
                        pl.when(t < CORES - 1)(functools.partial(act, r, b, place))

    def send(r, source, target, left, landed, place):
        pltpu.make_async_remote_copy(
            src_ref=source,
            dst_ref=target,
            send_sem=left,
            recv_sem=landed,
            device_id=place,
            device_id_type=MESH,
        ).start()

    def to_outer(*items):
        for r in range(2):
            for phase, source, target in items:
                pltpu.make_async_copy(
                    source(r, my_b[r]), target.at[r, my_b[r]], recv_sem.at[r, phase]
                ).start()

        def act(r, b, place):
            for phase, source, target in items:
                send(
                    r,
                    source(r, b),
                    target.at[r, my_b[r]],
                    send_sem.at[r, phase],
                    recv_sem.at[r, phase],
                    place,
                )

        each_outer(act)

    def to_chunk(t, far_x, *items):
        @pl.when(t == 0)
        def _():
            for r in range(2):
                for left, source, target, landed in items:
                    pltpu.make_async_copy(
                        source.at[r, my_k[r]], target.at[r, my_k[r]], landed(r)
                    ).start()

        def act(r, k, place):
            for left, source, target, landed in items:
                send(r, source.at[r, k], target.at[r, my_k[r]], left(r), landed(r), place)

        each_plane(t, far_x, act)

    def both_ends(phase, source, target):
        return (
            lambda r: send_sem.at[r, phase],
            source,
            target,
            lambda r: recv_sem.at[r, phase],
        )

    def to_plane(phase, source, target):
        @pl.loop(0, across)
        def _(t):
            far_x = wrap(x + far_x_of(t), across)
            to_chunk(t, far_x, both_ends(phase, source, target))

    def arrived(r, phase, target):
        pltpu.make_async_copy(target.at[r], target.at[r], recv_sem.at[r, phase]).wait()

    def sent(r, phase, target):
        gone = target.at[r, pl.ds(1, target.shape[1] - 1)]
        pltpu.make_async_copy(gone, gone, send_sem.at[r, phase]).wait()

    barrier = pltpu.get_barrier_semaphore()

    def greet(r, index, place):
        pl.semaphore_signal(barrier, inc=1, device_id=place, device_id_type=MESH)

    each_outer(greet)

    @pl.loop(0, across)
    def _(t):
        each_plane(t, wrap(x + far_x_of(t), across), greet)

    copy_held = pltpu.make_async_copy(passages_ref, held, held_sem)
    copy_held.start()

    probes = probes_ref[...]
    fb_probe, fb_row = fb_probe_ref[...], fb_row_ref[...]
    position = iota((queries, probe_count), 1)
    wanted = jnp.ones((queries, probe_count), jnp.int32)
    for k in range(fb_count):
        wanted = jnp.where(position == fb_probe[:, k : k + 1], fb_row[:, k : k + 1] + 2, wanted)
    list_lane = iota((queries, lists), 1)
    named = jnp.zeros((queries, lists), jnp.int32)
    for j in range(probe_count):
        named = jnp.where(list_lane == probes[:, j : j + 1], wanted[:, j : j + 1], named)
    member = named > 0
    before = jnp.where(iota((queries, queries), 0) > iota((queries, queries), 1), 1.0, 0.0)
    rank = jnp.dot(
        before.astype(BF16),
        jnp.where(member, 1.0, 0.0).astype(BF16),
        preferred_element_type=F32,
    )
    code = (iota((queries, lists), 0) + 1) * 256 + named
    code = jnp.where(member, code, 0)
    for s in range(SLOTS):
        row = jnp.sum(jnp.where(rank == float(s), code, 0), axis=0, keepdims=True)
        table[0:1, s * lists : (s + 1) * lists] = row
    pl.semaphore_wait(barrier, 2 * (blocks - 1 + plane - 1))
    to_outer((0, lambda r, b: table, table_in))

    tiles = plane // per_tile
    list_of = [per_tile * (p % tiles) + p // tiles for p in range(plane)]
    sub_b = iota((blocks, SLOTS * lists), 0)
    sub_p, lane_l = iota((plane, lists), 0), iota((plane, lists), 1)
    far_k = per_tile * (sub_p % tiles) + sub_p // tiles
    lane_slab = iota((tiles, LANES), 1)
    contract_last = (((1,), (1,)), ((), ()))
    slot_codes, list_hots = [], []
    for r in range(2):
        arrived(r, 0, table_in)
        all_codes = jnp.zeros((blocks, SLOTS * lists), jnp.int32)
        for b in range(blocks):
            all_codes = jnp.where(sub_b == b, table_in[r, b], all_codes)
        all_codes = jnp.concatenate(
            [all_codes[:, s * lists : (s + 1) * lists] for s in range(SLOTS)], axis=0
        )
        far_o, far_column = far_k % ring, far_k // ring
        if r == 0:
            far_list = grp * members + far_o * across + far_column
        else:
            far_list = (far_o * CORES + c) * members + row_y + far_column
        list_hot = jnp.where(lane_l == far_list, 1.0, 0.0).astype(BF16)
        want = (all_codes & 255).astype(F32).astype(BF16)
        want_rows = lax.dot_general(
            list_hot,
            jnp.concatenate([want] * (LANES // slab), axis=0),
            contract_last,
            preferred_element_type=F32,
        )
        for p, k in enumerate(list_of):
            asked[r, k] = want_rows[p : p + 1]
        slot_codes.append((all_codes >> 8).astype(F32).astype(BF16))
        list_hots.append(list_hot)
    to_plane(1, asked, asked_in)

    first_of = (iota((slab, plane), 0) % blocks * queries).astype(F32)
    query_lane = iota((slab, held_queries), 1).astype(F32)
    sub_q = iota((held_queries, tile_lanes), 0).astype(F32)
    for r in range(2):
        column = lax.dot_general(
            slot_codes[r], list_hots[r], contract_last, preferred_element_type=F32
        )
        column = jnp.where(column > 0.0, first_of + column - 1.0, -1.0)
        for p, k in enumerate(list_of):
            select[r, k] = jnp.where(query_lane == column[:, p : p + 1], 1.0, 0.0).astype(BF16)
        rows_of = lax.dot_general(
            list_hots[r],
            jnp.concatenate([slot_codes[r]] * (LANES // slab), axis=0),
            contract_last,
            preferred_element_type=F32,
        )
        joined = rows_of[:tiles]
        for i in range(1, per_tile):
            joined = jnp.where(
                lane_slab // slab == i, rows_of[i * tiles : (i + 1) * tiles], joined
            )
        joined = jnp.where(
            joined > 0.0, (lane_slab % blocks * queries).astype(F32) + joined - 1.0, -1.0
        )
        for j in range(tiles):
            spread[r, :, j * tile_lanes : (j + 1) * tile_lanes] = jnp.where(
                sub_q == joined[j : j + 1, :tile_lanes], 1.0, 0.0
            ).astype(BF16)

    tile_source = iota((1, tile_lanes), 1) // slab
    copy_held.wait()

    def lane_tile(ref, r, j):
        row = ref[r, per_tile * j][:, :tile_lanes]
        for i in range(1, per_tile):
            row = jnp.where(tile_source == i, ref[r, per_tile * j + i][:, :tile_lanes], row)
        return row

    for r in range(2):
        arrived(r, 1, asked_in)
        first = held[0:TILE, r * half : (r + 1) * half]
        sub_row = (iota((TILE, tile_lanes), 0) + 2).astype(F32)
        for j in range(tiles):
            row = lane_tile(asked_in, r, j)
            hot = jnp.where(sub_row == row, 1.0, 0.0).astype(BF16)
            picked = lax.dot_general(
                hot, first, (((0,), (0,)), ((), ())), preferred_element_type=F32
            ).astype(BF16)
            found[r, per_tile * j : per_tile * (j + 1)] = picked.reshape(per_tile, slab, half)
    to_plane(2, found, found_in)

    for r in range(2):
        arrived(r, 2, found_in)
        total = jnp.dot(spread[r], found_in[r].reshape(slots, half), preferred_element_type=F32)
        fsum[r] = total.astype(BF16).reshape(blocks, queries, half)
    to_outer((3, lambda r, b: fsum.at[r, b], fsum_in))

    for r in range(2):
        arrived(r, 3, fsum_in)
        total = jnp.zeros((queries, half), F32)
        for b in range(blocks):
            total = total + fsum_in[r, b].astype(F32)
        own = queries_ref[:, r * half : (r + 1) * half].astype(F32)
        roc[r] = (ALPHA_WEIGHT * own + BETA_WEIGHT * (total / fb_count)).astype(BF16)
    to_outer((4, lambda r, b: roc.at[r], roc_in))

    for r in range(2):
        arrived(r, 4, roc_in)

    @pl.loop(0, across)
    def _(t):
        far_x = wrap(x + far_x_of(t), across)
        there = pl.ds(far_x * ring, ring)
        for r in range(2):
            picked = jnp.dot(
                select[r, there].reshape(chunk, held_queries),
                roc_in[r].reshape(held_queries, half),
                preferred_element_type=F32,
            )
            vec[r, there] = picked.astype(BF16).reshape(ring, slab, half)
        to_chunk(
            t,
            far_x,
            (lambda r: send_sem.at[r, 5], vec, vec_in, lambda r: vec_sem.at[r, x]),
        )

    scale = 3.0 / math.sqrt(width)
    live = tiles_ref[0] * TILE
    bits = slab // 2
    turn = iota((slab, LANES), 0) == iota((slab, LANES), 1) % slab
    term_lane = iota((chunk, LANES), 1)

    def swapped(index):
        o, s, low = index // slab, (index % slab) // bits, index % bits
        return (low // CORES) * slab + s * bits + o * CORES + low % CORES

    swap = jnp.where(
        iota((chunk, chunk), 0) == swapped(iota((chunk, chunk), 1)), 1.0, 0.0
    ).astype(BF16)

    @pl.loop(0, across)
    def _(t):
        far_x = wrap(x + wrap(across - far_x_of(t), across), across)
        there = pl.ds(far_x * ring, ring)
        for r in range(2):
            landed = vec_in.at[r, there]
            pltpu.make_async_copy(landed, landed, vec_sem.at[r, far_x]).wait()
        first = vec_in[0, there].reshape(chunk, half)
        second = jnp.dot(
            swap, vec_in[1, there].reshape(chunk, half), preferred_element_type=F32
        ).astype(BF16)
        scores = lax.dot_general(
            jnp.concatenate([first, second], axis=1),
            held[...],
            contract_last,
            preferred_element_type=F32,
        )
        scores = jnp.where(iota((chunk, rows), 1) < live, scores * scale, NEG_FILL)
        peak = jnp.max(scores, axis=1, keepdims=True)
        weights = jnp.exp(scores - peak)
        mass = jnp.sum(weights, axis=1, keepdims=True)
        value = jnp.dot(weights.astype(BF16), held[...], preferred_element_type=F32)
        value = (value / mass).astype(BF16)
        level = peak + jnp.log(mass)
        part[0, there] = value[:, :half].reshape(ring, slab, half)
        rest, terms = level, jnp.zeros((chunk, LANES), F32)
        for i in range(3):
            term = rest.astype(BF16).astype(F32)
            terms = jnp.where(term_lane == i, term, terms)
            rest = rest - term
        moved = jnp.dot(
            swap,
            jnp.concatenate([value[:, half:], terms.astype(BF16)], axis=1),
            preferred_element_type=F32,
        )
        part[1, there] = moved[:, :half].astype(BF16).reshape(ring, slab, half)
        levels = (level, jnp.sum(moved[:, half:], axis=1, keepdims=True))
        for o in range(ring):
            for r in range(2):
                near = levels[r][o * slab : (o + 1) * slab]
                row = jnp.sum(jnp.where(turn, near, 0.0), axis=0, keepdims=True)
                lse[r, far_x * ring + o] = row
        to_chunk(
            t,
            far_x,
            both_ends(7, lse, lse_in),
            both_ends(6, part, part_in),
        )

    square = iota((queries, LANES), 0) == iota((queries, LANES), 1)
    for r in range(2):
        arrived(r, 7, lse_in)
        levels = jnp.concatenate([lane_tile(lse_in, r, j) for j in range(tiles)], axis=1)
        mask = spread[r].astype(F32) > 0.0
        levels = jnp.where(mask, levels, NEG_FILL)
        top = jnp.max(levels, axis=1, keepdims=True)
        weights = jnp.where(mask, jnp.exp(levels - top), 0.0)
        total = jnp.sum(weights, axis=1, keepdims=True)
        high = weights.astype(BF16)
        low = (weights - high.astype(F32)).astype(BF16)
        arrived(r, 6, part_in)
        parts = part_in[r].reshape(slots, half)
        value = jnp.dot(high, parts, preferred_element_type=F32)
        value = value + jnp.dot(low, parts, preferred_element_type=F32)
        some = total > 0.0
        total = jnp.where(some, total, 1.0)
        comb[r] = (value / total).astype(BF16).reshape(blocks, queries, half)
        level = jnp.where(some, top + jnp.log(total), NEG_FILL)
        for b in range(blocks):
            near = level[b * queries : (b + 1) * queries]
            lse2[r, b] = jnp.sum(jnp.where(square, near, 0.0), axis=0, keepdims=True)
    to_outer((9, lambda r, b: lse2.at[r, b], lse2_in), (8, lambda r, b: comb.at[r, b], comb_in))

    for r in range(2):
        arrived(r, 9, lse2_in)
        level = [
            jnp.sum(jnp.where(square, lse2_in[r, b], 0.0), axis=1, keepdims=True)
            for b in range(blocks)
        ]
        top = functools.reduce(jnp.maximum, level)
        factor = [jnp.exp(v - top) for v in level]
        total = functools.reduce(jnp.add, factor)
        arrived(r, 8, comb_in)
        value = jnp.zeros((queries, half), F32)
        for b in range(blocks):
            value = value + factor[b] * comb_in[r, b].astype(F32)
        retrieved_ref[:, r * half : (r + 1) * half] = (value / total).astype(BF16)
        if r == 0:
            log_total = top + jnp.log(total)
            log_row = jnp.sum(jnp.where(square, log_total, 0.0), axis=0, keepdims=True)
            log_ref[...] = log_row[:, :queries]

    for r in range(2):
        for phase, target in (
            (0, table_in),
            (1, asked_in),
            (2, found_in),
            (3, fsum_in),
            (4, roc_in),
            (5, vec_in),
            (6, part_in),
            (7, lse_in),
            (8, comb_in),
            (9, lse2_in),
        ):
            sent(r, phase, target)


def per_device(queries, passages, list_tiles, probes, fb_probe, fb_row):
    groups, members = lax.axis_size("grp"), lax.axis_size("dev")
    rows, width = passages.shape
    query_rows, probe_count = probes.shape
    fb_count = fb_row.shape[1]
    sizes = (groups, members, rows, query_rows, probe_count, fb_count, width)
    lists, half, slab = groups * members, width // 2, SLOTS * groups
    across = members // (groups // CORES)
    slots = members * slab
    tile_lanes = min(LANES, slots)
    vmem = pl.BlockSpec(memory_space=pltpu.VMEM)
    plane_rows = pltpu.VMEM((2, members, slab, half), BF16)
    plane_float = pltpu.VMEM((2, members, 1, LANES), F32)
    outer_rows = pltpu.VMEM((2, groups, query_rows, half), BF16)
    outer_float = pltpu.VMEM((2, groups, 1, LANES), F32)
    retrieved, log_total = pl.pallas_call(
        functools.partial(kernel, sizes),
        out_shape=(
            jax.ShapeDtypeStruct((query_rows, width), BF16),
            jax.ShapeDtypeStruct((1, query_rows), F32),
        ),
        in_specs=[
            vmem,
            vmem,
            vmem,
            vmem,
            pl.BlockSpec(memory_space=pltpu.SMEM),
            pl.BlockSpec(memory_space=pl.ANY),
        ],
        out_specs=(vmem, vmem),
        scratch_shapes=[
            pltpu.VMEM((rows, width), BF16),
            pltpu.VMEM((1, SLOTS * lists), jnp.int32),
            pltpu.VMEM((2, groups, 1, SLOTS * lists), jnp.int32),
            plane_float,
            plane_float,
            pltpu.VMEM((2, members, slab, groups * query_rows), BF16),
            pltpu.VMEM((2, groups * query_rows, slots), BF16),
            plane_rows,
            plane_rows,
            outer_rows,
            outer_rows,
            pltpu.VMEM((2, query_rows, half), BF16),
            outer_rows,
            plane_rows,
            plane_rows,
            plane_rows,
            plane_rows,
            plane_float,
            plane_float,
            outer_rows,
            outer_rows,
            outer_float,
            outer_float,
            pltpu.SemaphoreType.DMA,
            pltpu.SemaphoreType.DMA((2, 10)),
            pltpu.SemaphoreType.DMA((2, 10)),
            pltpu.SemaphoreType.DMA((2, across)),
        ],
        compiler_params=pltpu.CompilerParams(
            collective_id=0, has_side_effects=True, vmem_limit_bytes=56 * 1024 * 1024
        ),
        name="probe_lists",
    )(queries, probes, fb_probe, fb_row, list_tiles, passages)
    return retrieved, log_total.reshape(query_rows)


def solution(mesh):
    spec = P(("grp", "dev"), None)
    flat = P(("grp", "dev"))
    return jax.shard_map(
        per_device,
        mesh=mesh,
        in_specs=(spec, spec, flat, spec, spec, spec),
        out_specs=(spec, flat),
        check_vma=False,
    )
```

```python
import functools
import math

import jax
import jax.numpy as jnp
from jax import lax
from jax.experimental import pallas as pl
from jax.experimental.pallas import tpu as pltpu
from jax.sharding import PartitionSpec as P

TILE = 128
SLOTS = 2
CORES = 2
LANES = 128
ALPHA_WEIGHT = 1.0
BETA_WEIGHT = 0.75
NEG_FILL = -1e30
F32 = jnp.float32
BF16 = jnp.bfloat16
MESH = pl.DeviceIdType.MESH


def iota(shape, dim):
    return lax.broadcasted_iota(jnp.int32, shape, dim)


def kernel(
    sizes,
    queries_ref,
    probes_ref,
    fb_probe_ref,
    fb_row_ref,
    tiles_ref,
    passages_ref,
    retrieved_ref,
    log_ref,
    held,
    table,
    table_in,
    asked,
    asked_in,
    select,
    spread,
    found,
    found_in,
    fsum,
    fsum_in,
    roc,
    roc_in,
    vec,
    vec_in,
    part,
    part_in,
    lse,
    lse_in,
    comb,
    comb_in,
    lse2,
    lse2_in,
    held_sem,
    send_sem,
    recv_sem,
    vec_sem,
):
    groups, members, rows, queries, probe_count, fb_count, width = sizes
    ring = groups // CORES
    across = members // ring
    lists = groups * members
    half = width // 2
    blocks = groups
    slab = SLOTS * blocks
    plane = members
    chunk = ring * slab
    held_queries = blocks * queries
    slots = plane * slab
    tile_lanes = min(LANES, slots)
    per_tile = tile_lanes // slab

    grp, dev = lax.axis_index("grp"), lax.axis_index("dev")
    z, c = grp // CORES, grp % CORES
    y, x = dev // across, dev % across
    my_b = (grp, y * CORES + c)
    my_k = (x * ring + y, x * ring + z)

    def wrap(index, n):
        return jnp.where(index >= n, index - n, index)

    steps = sorted(range(ring), key=lambda step: -min(step, ring - step))
    far_y = [wrap(y + step, ring) for step in steps]
    far_z = [wrap(z + step, ring) for step in steps]
    dev_y = [v * across for v in far_y]
    grp_z = [v * CORES for v in far_z]
    row_y, column_z = y * across, z * CORES

    def plane_place(r, n, far_x):
        if r == 0:
            return far_x * ring + far_y[n], (grp, dev_y[n] + far_x)
        return far_x * ring + far_z[n], (grp_z[n] + c, row_y + far_x)

    def outer_place(r, n, far_c):
        if r == 0:
            return grp_z[n] + far_c, (grp_z[n] + far_c, dev)
        return far_y[n] * CORES + far_c, (column_z + far_c, dev_y[n] + x)

    def far_x_of(t):
        if across == 4:
            return jnp.where(t == 0, 0, jnp.where(t == 1, 2, jnp.where(t == 2, 3, 1)))
        return t

    def each_plane(t, far_x, act):
        for n in range(ring):
            for r in range(2):
                k, place = plane_place(r, n, far_x)
                if n < ring - 1:
                    act(r, k, place)
                else:
                    pl.when(t > 0)(functools.partial(act, r, k, place))

    def each_outer(act, routes=(0, 1)):
        @pl.loop(0, CORES)
        def _(t):
            far_c = jnp.where(t == 0, 1 - c, c)
            for n in range(ring):
                for r in routes:
                    b, place = outer_place(r, n, far_c)
                    if n < ring - 1:
                        act(r, b, place)
                    else:
                        pl.when(t < CORES - 1)(functools.partial(act, r, b, place))

    def send(r, source, target, left, landed, place):
        pltpu.make_async_remote_copy(
            src_ref=source,
            dst_ref=target,
            send_sem=left,
            recv_sem=landed,
            device_id=place,
            device_id_type=MESH,
        ).start()

    def to_outer(*items, routes=(0, 1)):
        for r in routes:
            for phase, source, target in items:
                pltpu.make_async_copy(
                    source(r, my_b[r]), target.at[r, my_b[r]], recv_sem.at[r, phase]
                ).start()

        def act(r, b, place):
            for phase, source, target in items:
                send(
                    r,
                    source(r, b),
                    target.at[r, my_b[r]],
                    send_sem.at[r, phase],
                    recv_sem.at[r, phase],
                    place,
                )

        each_outer(act, routes)

    def to_chunk(t, far_x, *items):
        @pl.when(t == 0)
        def _():
            for r in range(2):
                for left, source, target, landed in items:
                    pltpu.make_async_copy(
                        source.at[r, my_k[r]], target.at[r, my_k[r]], landed(r)
                    ).start()

        def act(r, k, place):
            for left, source, target, landed in items:
                send(r, source.at[r, k], target.at[r, my_k[r]], left(r), landed(r), place)

        each_plane(t, far_x, act)

    def both_ends(phase, source, target):
        return (
            lambda r: send_sem.at[r, phase],
            source,
            target,
            lambda r: recv_sem.at[r, phase],
        )

    def to_plane(phase, source, target):
        @pl.loop(0, across)
        def _(t):
            far_x = wrap(x + far_x_of(t), across)
            to_chunk(t, far_x, both_ends(phase, source, target))

    def arrived(r, phase, target):
        pltpu.make_async_copy(target.at[r], target.at[r], recv_sem.at[r, phase]).wait()

    def sent(r, phase, target):
        gone = target.at[r, pl.ds(1, target.shape[1] - 1)]
        pltpu.make_async_copy(gone, gone, send_sem.at[r, phase]).wait()

    barrier = pltpu.get_barrier_semaphore()

    def greet(r, index, place):
        pl.semaphore_signal(barrier, inc=1, device_id=place, device_id_type=MESH)

    each_outer(greet)

    @pl.loop(0, across)
    def _(t):
        each_plane(t, wrap(x + far_x_of(t), across), greet)

    copy_held = pltpu.make_async_copy(passages_ref, held, held_sem)
    copy_held.start()

    probes = probes_ref[...]
    fb_probe, fb_row = fb_probe_ref[...], fb_row_ref[...]
    position = iota((queries, probe_count), 1)
    wanted = jnp.ones((queries, probe_count), jnp.int32)
    for k in range(fb_count):
        wanted = jnp.where(position == fb_probe[:, k : k + 1], fb_row[:, k : k + 1] + 2, wanted)
    list_lane = iota((queries, lists), 1)
    named = jnp.zeros((queries, lists), jnp.int32)
    for j in range(probe_count):
        named = jnp.where(list_lane == probes[:, j : j + 1], wanted[:, j : j + 1], named)
    member = named > 0
    before = jnp.where(iota((queries, queries), 0) > iota((queries, queries), 1), 1.0, 0.0)
    rank = jnp.dot(
        before.astype(BF16),
        jnp.where(member, 1.0, 0.0).astype(BF16),
        preferred_element_type=F32,
    )
    code = (iota((queries, lists), 0) + 1) * 256 + named
    code = jnp.where(member, code, 0)
    for s in range(SLOTS):
        row = jnp.sum(jnp.where(rank == float(s), code, 0), axis=0, keepdims=True)
        table[0:1, s * lists : (s + 1) * lists] = row
    pl.semaphore_wait(barrier, 2 * (blocks - 1 + plane - 1))
    to_outer((0, lambda r, b: table, table_in))

    tiles = plane // per_tile
    list_of = [per_tile * (p % tiles) + p // tiles for p in range(plane)]
    sub_b = iota((blocks, SLOTS * lists), 0)
    sub_p, lane_l = iota((plane, lists), 0), iota((plane, lists), 1)
    far_k = per_tile * (sub_p % tiles) + sub_p // tiles
    lane_slab = iota((tiles, LANES), 1)
    contract_last = (((1,), (1,)), ((), ()))
    slot_codes, list_hots = [], []
    for r in range(2):
        arrived(r, 0, table_in)
        all_codes = jnp.zeros((blocks, SLOTS * lists), jnp.int32)
        for b in range(blocks):
            all_codes = jnp.where(sub_b == b, table_in[r, b], all_codes)
        all_codes = jnp.concatenate(
            [all_codes[:, s * lists : (s + 1) * lists] for s in range(SLOTS)], axis=0
        )
        far_o, far_column = far_k % ring, far_k // ring
        if r == 0:
            far_list = grp * members + far_o * across + far_column
        else:
            far_list = (far_o * CORES + c) * members + row_y + far_column
        list_hot = jnp.where(lane_l == far_list, 1.0, 0.0).astype(BF16)
        want = (all_codes & 255).astype(F32).astype(BF16)
        want_rows = lax.dot_general(
            list_hot,
            jnp.concatenate([want] * (LANES // slab), axis=0),
            contract_last,
            preferred_element_type=F32,
        )
        for p, k in enumerate(list_of):
            asked[r, k] = want_rows[p : p + 1]
        slot_codes.append((all_codes >> 8).astype(F32).astype(BF16))
        list_hots.append(list_hot)
    to_plane(1, asked, asked_in)

    first_of = (iota((slab, plane), 0) % blocks * queries).astype(F32)
    query_lane = iota((slab, held_queries), 1).astype(F32)
    sub_q = iota((held_queries, tile_lanes), 0).astype(F32)
    for r in range(2):
        column = lax.dot_general(
            slot_codes[r], list_hots[r], contract_last, preferred_element_type=F32
        )
        column = jnp.where(column > 0.0, first_of + column - 1.0, -1.0)
        for p, k in enumerate(list_of):
            select[r, k] = jnp.where(query_lane == column[:, p : p + 1], 1.0, 0.0).astype(BF16)
        rows_of = lax.dot_general(
            list_hots[r],
            jnp.concatenate([slot_codes[r]] * (LANES // slab), axis=0),
            contract_last,
            preferred_element_type=F32,
        )
        joined = rows_of[:tiles]
        for i in range(1, per_tile):
            joined = jnp.where(
                lane_slab // slab == i, rows_of[i * tiles : (i + 1) * tiles], joined
            )
        joined = jnp.where(
            joined > 0.0, (lane_slab % blocks * queries).astype(F32) + joined - 1.0, -1.0
        )
        for j in range(tiles):
            spread[r, :, j * tile_lanes : (j + 1) * tile_lanes] = jnp.where(
                sub_q == joined[j : j + 1, :tile_lanes], 1.0, 0.0
            ).astype(BF16)

    tile_source = iota((1, tile_lanes), 1) // slab
    copy_held.wait()

    def lane_tile(ref, r, j):
        row = ref[r, per_tile * j][:, :tile_lanes]
        for i in range(1, per_tile):
            row = jnp.where(tile_source == i, ref[r, per_tile * j + i][:, :tile_lanes], row)
        return row

    for r in range(2):
        arrived(r, 1, asked_in)
        first = held[0:TILE, r * half : (r + 1) * half]
        sub_row = (iota((TILE, tile_lanes), 0) + 2).astype(F32)
        for j in range(tiles):
            row = lane_tile(asked_in, r, j)
            hot = jnp.where(sub_row == row, 1.0, 0.0).astype(BF16)
            picked = lax.dot_general(
                hot, first, (((0,), (0,)), ((), ())), preferred_element_type=F32
            ).astype(BF16)
            found[r, per_tile * j : per_tile * (j + 1)] = picked.reshape(per_tile, slab, half)
    to_plane(2, found, found_in)

    for r in range(2):
        arrived(r, 2, found_in)
        total = jnp.dot(spread[r], found_in[r].reshape(slots, half), preferred_element_type=F32)
        fsum[r] = total.astype(BF16).reshape(blocks, queries, half)
        to_outer((3, lambda r, b: fsum.at[r, b], fsum_in), routes=(r,))

    for r in range(2):
        arrived(r, 3, fsum_in)
        total = jnp.zeros((queries, half), F32)
        for b in range(blocks):
            total = total + fsum_in[r, b].astype(F32)
        own = queries_ref[:, r * half : (r + 1) * half].astype(F32)
        roc[r] = (ALPHA_WEIGHT * own + BETA_WEIGHT * (total / fb_count)).astype(BF16)
        to_outer((4, lambda r, b: roc.at[r], roc_in), routes=(r,))

    for r in range(2):
        arrived(r, 4, roc_in)

    @pl.loop(0, across)
    def _(t):
        far_x = wrap(x + far_x_of(t), across)
        there = pl.ds(far_x * ring, ring)
        for r in range(2):
            picked = jnp.dot(
                select[r, there].reshape(chunk, held_queries),
                roc_in[r].reshape(held_queries, half),
                preferred_element_type=F32,
            )
            vec[r, there] = picked.astype(BF16).reshape(ring, slab, half)
        to_chunk(
            t,
            far_x,
            (lambda r: send_sem.at[r, 5], vec, vec_in, lambda r: vec_sem.at[r, x]),
        )

    scale = 3.0 / math.sqrt(width)
    live = tiles_ref[0] * TILE
    bits = slab // 2
    turn = iota((slab, LANES), 0) == iota((slab, LANES), 1) % slab
    term_lane = iota((chunk, LANES), 1)

    def swapped(index):
        o, s, low = index // slab, (index % slab) // bits, index % bits
        return (low // CORES) * slab + s * bits + o * CORES + low % CORES

    swap = jnp.where(
        iota((chunk, chunk), 0) == swapped(iota((chunk, chunk), 1)), 1.0, 0.0
    ).astype(BF16)

    @pl.loop(0, across)
    def _(t):
        far_x = wrap(x + wrap(across - far_x_of(t), across), across)
        there = pl.ds(far_x * ring, ring)
        for r in range(2):
            landed = vec_in.at[r, there]
            pltpu.make_async_copy(landed, landed, vec_sem.at[r, far_x]).wait()
        first = vec_in[0, there].reshape(chunk, half)
        second = jnp.dot(
            swap, vec_in[1, there].reshape(chunk, half), preferred_element_type=F32
        ).astype(BF16)
        scores = lax.dot_general(
            jnp.concatenate([first, second], axis=1),
            held[...],
            contract_last,
            preferred_element_type=F32,
        )
        scores = jnp.where(iota((chunk, rows), 1) < live, scores * scale, NEG_FILL)
        peak = jnp.max(scores, axis=1, keepdims=True)
        weights = jnp.exp(scores - peak)
        mass = jnp.sum(weights, axis=1, keepdims=True)
        value = jnp.dot(weights.astype(BF16), held[...], preferred_element_type=F32)
        value = (value / mass).astype(BF16)
        level = peak + jnp.log(mass)
        part[0, there] = value[:, :half].reshape(ring, slab, half)
        rest, terms = level, jnp.zeros((chunk, LANES), F32)
        for i in range(3):
            term = rest.astype(BF16).astype(F32)
            terms = jnp.where(term_lane == i, term, terms)
            rest = rest - term
        moved = jnp.dot(
            swap,
            jnp.concatenate([value[:, half:], terms.astype(BF16)], axis=1),
            preferred_element_type=F32,
        )
        part[1, there] = moved[:, :half].astype(BF16).reshape(ring, slab, half)
        levels = (level, jnp.sum(moved[:, half:], axis=1, keepdims=True))
        for o in range(ring):
            for r in range(2):
                near = levels[r][o * slab : (o + 1) * slab]
                row = jnp.sum(jnp.where(turn, near, 0.0), axis=0, keepdims=True)
                lse[r, far_x * ring + o] = row
        to_chunk(
            t,
            far_x,
            both_ends(7, lse, lse_in),
            both_ends(6, part, part_in),
        )

    square = iota((queries, LANES), 0) == iota((queries, LANES), 1)
    for r in range(2):
        arrived(r, 7, lse_in)
        levels = jnp.concatenate([lane_tile(lse_in, r, j) for j in range(tiles)], axis=1)
        mask = spread[r].astype(F32) > 0.0
        levels = jnp.where(mask, levels, NEG_FILL)
        top = jnp.max(levels, axis=1, keepdims=True)
        weights = jnp.where(mask, jnp.exp(levels - top), 0.0)
        total = jnp.sum(weights, axis=1, keepdims=True)
        high = weights.astype(BF16)
        low = (weights - high.astype(F32)).astype(BF16)
        arrived(r, 6, part_in)
        parts = part_in[r].reshape(slots, half)
        value = jnp.dot(high, parts, preferred_element_type=F32)
        value = value + jnp.dot(low, parts, preferred_element_type=F32)
        some = total > 0.0
        total = jnp.where(some, total, 1.0)
        comb[r] = (value / total).astype(BF16).reshape(blocks, queries, half)
        level = jnp.where(some, top + jnp.log(total), NEG_FILL)
        for b in range(blocks):
            near = level[b * queries : (b + 1) * queries]
            lse2[r, b] = jnp.sum(jnp.where(square, near, 0.0), axis=0, keepdims=True)
        to_outer(
            (9, lambda r, b: lse2.at[r, b], lse2_in),
            (8, lambda r, b: comb.at[r, b], comb_in),
            routes=(r,),
        )

    for r in range(2):
        arrived(r, 9, lse2_in)
        level = [
            jnp.sum(jnp.where(square, lse2_in[r, b], 0.0), axis=1, keepdims=True)
            for b in range(blocks)
        ]
        top = functools.reduce(jnp.maximum, level)
        factor = [jnp.exp(v - top) for v in level]
        total = functools.reduce(jnp.add, factor)
        arrived(r, 8, comb_in)
        value = jnp.zeros((queries, half), F32)
        for b in range(blocks):
            value = value + factor[b] * comb_in[r, b].astype(F32)
        retrieved_ref[:, r * half : (r + 1) * half] = (value / total).astype(BF16)
        if r == 0:
            log_total = top + jnp.log(total)
            log_row = jnp.sum(jnp.where(square, log_total, 0.0), axis=0, keepdims=True)
            log_ref[...] = log_row[:, :queries]

    for r in range(2):
        for phase, target in (
            (0, table_in),
            (1, asked_in),
            (2, found_in),
            (3, fsum_in),
            (4, roc_in),
            (5, vec_in),
            (6, part_in),
            (7, lse_in),
            (8, comb_in),
            (9, lse2_in),
        ):
            sent(r, phase, target)


def per_device(queries, passages, list_tiles, probes, fb_probe, fb_row):
    groups, members = lax.axis_size("grp"), lax.axis_size("dev")
    rows, width = passages.shape
    query_rows, probe_count = probes.shape
    fb_count = fb_row.shape[1]
    sizes = (groups, members, rows, query_rows, probe_count, fb_count, width)
    lists, half, slab = groups * members, width // 2, SLOTS * groups
    across = members // (groups // CORES)
    slots = members * slab
    tile_lanes = min(LANES, slots)
    vmem = pl.BlockSpec(memory_space=pltpu.VMEM)
    plane_rows = pltpu.VMEM((2, members, slab, half), BF16)
    plane_float = pltpu.VMEM((2, members, 1, LANES), F32)
    outer_rows = pltpu.VMEM((2, groups, query_rows, half), BF16)
    outer_float = pltpu.VMEM((2, groups, 1, LANES), F32)
    retrieved, log_total = pl.pallas_call(
        functools.partial(kernel, sizes),
        out_shape=(
            jax.ShapeDtypeStruct((query_rows, width), BF16),
            jax.ShapeDtypeStruct((1, query_rows), F32),
        ),
        in_specs=[
            vmem,
            vmem,
            vmem,
            vmem,
            pl.BlockSpec(memory_space=pltpu.SMEM),
            pl.BlockSpec(memory_space=pl.ANY),
        ],
        out_specs=(vmem, vmem),
        scratch_shapes=[
            pltpu.VMEM((rows, width), BF16),
            pltpu.VMEM((1, SLOTS * lists), jnp.int32),
            pltpu.VMEM((2, groups, 1, SLOTS * lists), jnp.int32),
            plane_float,
            plane_float,
            pltpu.VMEM((2, members, slab, groups * query_rows), BF16),
            pltpu.VMEM((2, groups * query_rows, slots), BF16),
            plane_rows,
            plane_rows,
            outer_rows,
            outer_rows,
            pltpu.VMEM((2, query_rows, half), BF16),
            outer_rows,
            plane_rows,
            plane_rows,
            plane_rows,
            plane_rows,
            plane_float,
            plane_float,
            outer_rows,
            outer_rows,
            outer_float,
            outer_float,
            pltpu.SemaphoreType.DMA,
            pltpu.SemaphoreType.DMA((2, 10)),
            pltpu.SemaphoreType.DMA((2, 10)),
            pltpu.SemaphoreType.DMA((2, across)),
        ],
        compiler_params=pltpu.CompilerParams(
            collective_id=0, has_side_effects=True, vmem_limit_bytes=56 * 1024 * 1024
        ),
        name="probe_lists",
    )(queries, probes, fb_probe, fb_row, list_tiles, passages)
    return retrieved, log_total.reshape(query_rows)


def solution(mesh):
    spec = P(("grp", "dev"), None)
    flat = P(("grp", "dev"))
    return jax.shard_map(
        per_device,
        mesh=mesh,
        in_specs=(spec, spec, flat, spec, spec, spec),
        out_specs=(spec, flat),
        check_vma=False,
    )
```
